512 devices in a mesh: mem: 32 (over y_hi, z), dp: 16 (over x, y_lo, core).
Axes of the slice: x: 4, y: 4 (y_hi: 2, y_lo: 2; y = y_hi * 2 + y_lo), z: 16, core: 2. Of those that a mesh axis runs over, the one named last changes fastest.
Arguments:
- query_vectors: bfloat16 [65536, 256], P(('mem', 'dp')), may hold values from -2 to 2
- item_vectors: bfloat16 [65536, 256], P(('mem', 'dp')), may hold values from -1.5 to 1.5
- negative_vectors: bfloat16 [32768, 256], P(('mem', 'dp')), may hold values from -1.5 to 1.5
- item_ids: int32 [65536], P(('mem', 'dp')), may hold values from 0 to 65535, as said below
- negative_ids: int32 [32768], P(('mem', 'dp')), may hold values from 0 to 65535, as said below
- negative_counts: int32 [32768], P(('mem', 'dp')), may hold values from 1 to 4
- memory: bfloat16 [16, 32768, 256], P('dp', 'mem'), may hold values from -2 to 2
- owners: int32 [65536, 1], P(('mem', 'dp')), may hold values from 0 to 31, as said below
- memory_slots: int32 [65536], P(('mem', 'dp')), may hold values from 0 to 1023
Outputs:
- query_loss: float32 [65536], P(('mem', 'dp'))
- query_grad: float32 [65536, 256], P(('mem', 'dp'))
- item_grad: float32 [65536, 256], P(('mem', 'dp'))
- negative_grad: float32 [32768, 256], P(('mem', 'dp'))
- new_memory: bfloat16 [16, 32768, 256], P('dp', 'mem')
The draws below stay inside these ranges and needn't reach their ends.
Inputs may be any that keep to these rules, and one draw needn't show every extreme that they name: `item_ids`: catalogue ids; every binary octave of ids is about equally likely. `negative_ids`: catalogue ids; every binary octave of ids is about equally likely. `owners`: among the 128 items of one device no owner is named more than 8 times; for every dp index one owner is named exactly 8 times by each device with that dp index.
All inputs are finite; a program needn't handle non-finite values.
Results may differ from the reference program's by a relative error of at most 0.003.
Values may be sent and summed in bfloat16 or wider, within the bound.
No kernel may reach another device: no remote copies, remote signals or barrier semaphores. Data moves between devices by JAX's collectives and lax.ppermute only.
A program may use at most 64 MiB of HBM per device.

```python
import math
import jax
import jax.numpy as jnp
from jax import lax

D = 256
Q_DEV = 128
MEM_DEV = 1024
ITEMS = 65536
QUERIES = 65536
B_GRP = 2048
NEG_GRP = 1024
NEGS = 32768
MEM_ROWS = 32768
N_MEM = 32
N_DP = 16


def draw_query_vectors(key, part):
    key = jax.random.fold_in(key, 3)
    values = 0.25 * jax.random.truncated_normal(key, -4.0, 4.0, (QUERIES, D), jnp.float32)
    return values.astype(jnp.bfloat16)


def draw_memory(key, part):
    key = jax.random.fold_in(key, 7)
    shard_place = jnp.arange(N_MEM, dtype=jnp.float32) / max(N_MEM - 1, 1)
    rising = (1.0 + 0.8 * shard_place)[None, :, None, None]
    values = 0.25 * jax.random.truncated_normal(key, -4.0, 4.0, (N_DP, N_MEM, MEM_DEV, D), jnp.float32) * rising
    return values.reshape(N_DP, MEM_ROWS, D).astype(jnp.bfloat16)


def octave_ids(key, count):
    octave_key, offset_key = jax.random.split(key)
    octaves = jax.random.randint(octave_key, (count,), 0, ITEMS.bit_length() - 1)
    widths = jnp.left_shift(jnp.ones((count,), jnp.int32), octaves)
    offsets = jax.random.randint(offset_key, (count,), 0, widths)
    return widths - 1 + offsets


def draw_item_ids(key, part):
    key = jax.random.fold_in(key, 13)
    return octave_ids(key, QUERIES)


def draw_negative_ids(key, part):
    key = jax.random.fold_in(key, 17)
    return octave_ids(key, NEGS)


def draw_owners(key, part):
    key = jax.random.fold_in(key, 19)
    capacity = max(2, 2 * Q_DEV // N_MEM)
    hot_key, rank_key, score_key, order_key = jax.random.split(key, 4)
    hottest = jax.random.randint(hot_key, (N_DP,), 0, N_MEM)
    ranking = jax.vmap(lambda single: jax.random.permutation(single, N_MEM))(jax.random.split(rank_key, N_DP))
    pool_owner = jnp.arange(N_MEM * capacity, dtype=jnp.int32) // capacity
    leaning = 1024 * (N_MEM - ranking) // N_MEM
    noise = jax.random.randint(score_key, (N_MEM, N_DP, N_MEM * capacity), 0, 1024)
    scores = noise + leaning[:, pool_owner][None, :, :]
    scores = jnp.where(pool_owner[None, None, :] == hottest[None, :, None], -1, scores)
    scores = scores * (N_MEM * capacity) + jnp.arange(N_MEM * capacity, dtype=jnp.int32)
    picked = lax.top_k(scores, Q_DEV - capacity)[1]
    others = pool_owner[picked]
    hot_rows = jnp.broadcast_to(hottest[None, :, None], (N_MEM, N_DP, capacity)).astype(jnp.int32)
    owner_rows = jnp.concatenate([hot_rows, others], axis=2)
    shuffles = jax.vmap(lambda single: jax.random.permutation(single, Q_DEV))(jax.random.split(order_key, N_MEM * N_DP))
    owner_rows = jnp.take_along_axis(owner_rows, shuffles.reshape(N_MEM, N_DP, Q_DEV), axis=2)
    return owner_rows.reshape(QUERIES, 1)


def place_ends(result, own_key, least, largest):
    longest = result.shape.index(max(result.shape))
    spots = []
    for shift in (0, 1):
        where = [jax.random.randint(jax.random.fold_in(own_key, axis), (), 0, length) for axis, length in enumerate(result.shape)]
        where[longest] = (where[longest] + shift) % result.shape[longest]
        spots.append(tuple(where))
    return result.at[spots[0]].set(least).at[spots[1]].set(largest)


def steps_of(rng, shape, pieces, smallest, high):
    def one(axis_at, shards_of):
        draws = jax.random.uniform(jax.random.fold_in(jax.random.fold_in(rng, 6), axis_at), (shards_of,), jnp.float32, smallest / len(pieces), high / len(pieces))
        return jnp.repeat(jnp.exp(draws), shape[axis_at] // shards_of).reshape((-1,) + (1,) * (len(shape) - axis_at - 1))

    level = one(*pieces[0])
    for cut in pieces[1:]:
        level = level * one(*cut)
    return level


def centred(key, extent, width, reach, pieces=(), held_as=jnp.bfloat16):
    gain = steps_of(key, extent, pieces, -0.22, 0.18) if pieces else 1.0
    values = jax.random.normal(key, extent, jnp.float32) * width * gain
    return jnp.minimum(jnp.maximum(values, -reach), reach).astype(held_as)


def setup_inputs(seed: int = 0) -> dict:
    splits = jax.random.split(jax.random.key(seed), 10)
    query_vectors = draw_query_vectors(jax.random.fold_in(splits[9], 71), 0)
    item_vectors = centred(splits[1], (QUERIES, D), 0.25, 1.5, ((0, 512),))
    negative_vectors = centred(splits[2], (NEGS, D), 0.25, 1.5, ((0, 512),))
    item_ids = draw_item_ids(jax.random.fold_in(splits[9], 71), 0)
    negative_ids = draw_negative_ids(jax.random.fold_in(splits[9], 71), 0)
    negative_counts = place_ends(jax.random.randint(splits[5], (NEGS,), 1, 5), jax.random.fold_in(splits[5], 1), 1, 4).astype(jnp.int32)
    memory = draw_memory(jax.random.fold_in(splits[9], 71), 0)
    owners = draw_owners(jax.random.fold_in(splits[9], 71), 0)
    memory_slots = place_ends(jax.random.randint(splits[8], (QUERIES,), 0, MEM_DEV), jax.random.fold_in(splits[8], 1), 0, MEM_DEV - 1).astype(jnp.int32)
    return {"query_vectors": query_vectors, "item_vectors": item_vectors, "negative_vectors": negative_vectors, "item_ids": item_ids, "negative_ids": negative_ids, "negative_counts": negative_counts, "memory": memory, "owners": owners, "memory_slots": memory_slots}


def sample_chance(identities):
    return jnp.log1p(1.0 / (identities.astype(jnp.float32) + 1.0)) / math.log(ITEMS + 1)


def inner_products(left, right):
    return lax.dot_general(left, right, (((1,), (1,)), ((), ())), preferred_element_type=jnp.float32)


def column_sums(weights, vectors):
    return lax.dot_general(weights, vectors, (((0,), (0,)), ((), ())), preferred_element_type=jnp.float32)


def place_items(memory_rows, candidates, target_rows, arrival):
    row_count = memory_rows.shape[0]
    entry_count = target_rows.shape[0]
    latest = jnp.full((row_count,), -1, jnp.int32).at[target_rows].max(arrival)
    winners = (arrival >= 0) & (arrival == latest[target_rows])
    positions = jnp.where(winners, jnp.arange(entry_count, dtype=jnp.int32), 0)
    chosen = jnp.zeros((row_count,), jnp.int32).at[target_rows].max(positions)
    fresh_rows = jnp.take(candidates, chosen, axis=0)
    return jnp.where((latest >= 0)[:, None], fresh_rows, memory_rows)


def reference(query_vectors, item_vectors, negative_vectors, item_ids, negative_ids, negative_counts, memory, owners, memory_slots):
    batch_shift = (-jnp.log(B_GRP * sample_chance(item_ids))).reshape(N_MEM, B_GRP)
    negative_shift = (jnp.log(negative_counts.astype(jnp.float32)) - jnp.log(NEG_GRP * sample_chance(negative_ids))).reshape(N_MEM, NEG_GRP)
    grouped_queries = query_vectors.reshape(N_MEM, N_DP, Q_DEV, D)
    grouped_items = item_vectors.reshape(N_MEM, B_GRP, D)
    grouped_negatives = negative_vectors.reshape(N_MEM, NEG_GRP, D)

    def one_group(group_args):
        group_queries, group_items, group_negatives, item_shift, neg_shift = group_args

        def one_block(sums, block_args):
            item_sums, negative_sums = sums
            query_block, memory_column, column = block_args
            batch_logits = inner_products(query_block, group_items) + item_shift[None, :]
            negative_logits = inner_products(query_block, group_negatives) + neg_shift[None, :]
            memory_logits = inner_products(query_block, memory_column)
            highest = jnp.maximum(jnp.maximum(jnp.max(batch_logits, axis=1), jnp.max(negative_logits, axis=1)), jnp.max(memory_logits, axis=1))
            exp_total = (jnp.sum(jnp.exp(batch_logits - highest[:, None]), axis=1)
                         + jnp.sum(jnp.exp(negative_logits - highest[:, None]), axis=1)
                         + jnp.sum(jnp.exp(memory_logits - highest[:, None]), axis=1))
            log_total = highest + jnp.log(exp_total)
            own_logits = jnp.diagonal(lax.dynamic_slice_in_dim(batch_logits, column * Q_DEV, Q_DEV, 1))
            own_items = lax.dynamic_slice_in_dim(group_items, column * Q_DEV, Q_DEV, 0)
            batch_weights = jnp.exp(batch_logits - log_total[:, None]).astype(jnp.bfloat16)
            negative_weights = jnp.exp(negative_logits - log_total[:, None]).astype(jnp.bfloat16)
            memory_weights = jnp.exp(memory_logits - log_total[:, None]).astype(jnp.bfloat16)
            query_grad = (jnp.dot(batch_weights, group_items, preferred_element_type=jnp.float32)
                          + jnp.dot(negative_weights, group_negatives, preferred_element_type=jnp.float32)
                          + jnp.dot(memory_weights, memory_column, preferred_element_type=jnp.float32)
                          - own_items.astype(jnp.float32))
            item_sums = item_sums + column_sums(batch_weights, query_block)
            negative_sums = negative_sums + column_sums(negative_weights, query_block)
            return (item_sums, negative_sums), (log_total - own_logits, query_grad)

        start_sums = (jnp.zeros((B_GRP, D), jnp.float32), jnp.zeros((NEG_GRP, D), jnp.float32))
        (item_sums, negative_sums), (losses, grads) = lax.scan(
            one_block, start_sums, (group_queries, memory, jnp.arange(N_DP, dtype=jnp.int32)))
        item_grad = item_sums - group_queries.reshape(B_GRP, D).astype(jnp.float32)
        return losses, grads, item_grad, negative_sums

    losses, grads, item_grads, negative_grads = lax.map(
        one_group, (grouped_queries, grouped_items, grouped_negatives, batch_shift, negative_shift))

    column_items = jnp.transpose(item_vectors.reshape(N_MEM, N_DP, Q_DEV, D), (1, 0, 2, 3)).reshape(N_DP, N_MEM * Q_DEV, D)
    column_owners = jnp.transpose(owners.reshape(N_MEM, N_DP, Q_DEV), (1, 0, 2)).reshape(N_DP, N_MEM * Q_DEV)
    column_slots = jnp.transpose(memory_slots.reshape(N_MEM, N_DP, Q_DEV), (1, 0, 2)).reshape(N_DP, N_MEM * Q_DEV)
    target_rows = column_owners * MEM_DEV + column_slots
    arrival = jnp.arange(N_MEM * Q_DEV, dtype=jnp.int32)
    new_memory = jax.vmap(place_items, in_axes=(0, 0, 0, None))(memory, column_items, target_rows, arrival)
    return (losses.reshape(QUERIES), grads.reshape(QUERIES, D), item_grads.reshape(QUERIES, D),
            negative_grads.reshape(NEGS, D), new_memory)
```

```python
import math

import jax
import jax.numpy as jnp
from jax import lax
from jax.experimental import pallas as pl
from jax.experimental.pallas import tpu as pltpu
from jax.sharding import Mesh, PartitionSpec as P

ITEMS = 65536
BF16 = jnp.bfloat16
F32 = jnp.float32
VMEM_LIMIT = 56 * 1024 * 1024


def sample_chance(identities):
    return jnp.log1p(1.0 / (identities.astype(F32) + 1.0)) / math.log(ITEMS + 1)


def dot_rows(left, right):
    return lax.dot_general(left, right, (((1,), (1,)), ((), ())), preferred_element_type=F32)


def dot_plain(left, right):
    return jnp.dot(left, right, preferred_element_type=F32)


def eye(size):
    return lax.broadcasted_iota(jnp.int32, (size, size), 0) == lax.broadcasted_iota(
        jnp.int32, (size, size), 1
    )


def to_row(column):
    return jnp.sum(jnp.where(eye(column.shape[0]), column, 0), axis=0, keepdims=True)


def to_column(row):
    return jnp.sum(jnp.where(eye(row.shape[1]), row, 0), axis=1, keepdims=True)


def call(kernel, out_shape, name, **more):
    return pl.pallas_call(
        kernel,
        out_shape=out_shape,
        name=name,
        compiler_params=pltpu.CompilerParams(vmem_limit_bytes=VMEM_LIMIT),
        **more,
    )


def prepare_kernel(
    capacity, q_ref, it_ref, ng_ref, sh_ref, own_col_ref, own_row_ref, slot_ref, block_ref, out_ref
):
    rows, keys = q_ref.shape[0], it_ref.shape[0] + ng_ref.shape[0]
    block_ref[0:rows, :] = q_ref[...]
    block_ref[rows : 2 * rows, :] = it_ref[...]
    block_ref[2 * rows : rows + keys, :] = ng_ref[...]
    shift = sh_ref[...]
    high = shift.astype(BF16)
    rest = shift - high.astype(F32)
    middle = rest.astype(BF16)
    low = (rest - middle.astype(F32)).astype(BF16)
    extra = block_ref.shape[0] - rows - keys
    place = lax.broadcasted_iota(jnp.int32, (extra, keys), 0)
    stacked = jnp.where(
        place == 0,
        high.astype(F32),
        jnp.where(place == 1, middle.astype(F32), jnp.where(place == 2, low.astype(F32), 0.0)),
    )
    block_ref[rows + keys :, :] = jnp.zeros((extra, block_ref.shape[1]), BF16)
    block_ref[rows + keys :, 0:keys] = stacked.astype(BF16)

    count = it_ref.shape[0]
    own_col, own_row = own_col_ref[...], own_row_ref[...]
    earlier = lax.broadcasted_iota(jnp.int32, (count, count), 0) < lax.broadcasted_iota(
        jnp.int32, (count, count), 1
    )
    rank = jnp.sum(
        jnp.where(jnp.logical_and(own_col == own_row, earlier), 1.0, 0.0), axis=0, keepdims=True
    )
    target = own_row * capacity + rank.astype(jnp.int32)
    places = out_ref.shape[0]
    chosen = jnp.where(
        lax.broadcasted_iota(jnp.int32, (places, count), 0) == target, 1.0, 0.0
    ).astype(BF16)
    slot = slot_ref[...]
    lane = lax.broadcasted_iota(jnp.int32, (count, 128), 1)
    details = jnp.where(
        lane == 0, slot >> 5, jnp.where(lane == 1, slot & 31, jnp.where(lane == 2, 1, 0))
    )
    width = it_ref.shape[1]
    out_ref[:, 0:width] = dot_plain(chosen, it_ref[...]).astype(BF16)
    out_ref[:, width:] = dot_plain(chosen, details.astype(F32).astype(BF16)).astype(BF16)


def update_kernel(got_ref, mem_ref, new_ref):
    places, width = got_ref.shape[0], mem_ref.shape[1]
    rows = mem_ref.shape[0]
    details = jnp.transpose(got_ref[:, width:].astype(F32))
    slot = details[0:1, :] * 32.0 + details[1:2, :]
    slot = jnp.where(details[2:3, :] > 0.5, slot, -1.0).astype(jnp.int32)
    entry = lax.broadcasted_iota(jnp.int32, (1, places), 1).astype(F32)
    step = 256
    for start in range(0, rows, step):
        row = lax.broadcasted_iota(jnp.int32, (step, places), 0) + start
        latest = jnp.max(jnp.where(row == slot, entry, -1.0), axis=1, keepdims=True)
        chosen = jnp.where(entry == latest, 1.0, 0.0).astype(BF16)
        fresh = dot_plain(chosen, got_ref[:, 0:width])
        old = mem_ref[start : start + step, :].astype(F32)
        new_ref[start : start + step, :] = jnp.where(latest >= 0.0, fresh, old).astype(BF16)


def memory_kernel(*refs):
    q_ref, *mem_refs, out_ref, lse_ref, s_ref = refs
    step = 512
    pieces = [(ref, at) for ref in mem_refs for at in range(0, ref.shape[0], step)]
    q = q_ref[...]
    highest = None
    for n, (ref, at) in enumerate(pieces):
        s = dot_rows(q, ref[at : at + step, :])
        s_ref[:, n * step : (n + 1) * step] = s
        for lane in range(0, step, 128):
            part = s[:, lane : lane + 128]
            highest = part if highest is None else jnp.maximum(highest, part)
    top = jnp.max(highest, axis=1, keepdims=True)
    total = jnp.zeros((q.shape[0], 128), F32)
    acc = jnp.zeros(q.shape, F32)
    for n, (ref, at) in enumerate(pieces):
        p = jnp.exp(s_ref[:, n * step : (n + 1) * step] - top)
        for lane in range(0, step, 128):
            total = total + p[:, lane : lane + 128]
        acc = acc + dot_plain(p.astype(BF16), ref[at : at + step, :])
    total = jnp.sum(total, axis=1, keepdims=True)
    out_ref[...] = (acc / total).astype(BF16)
    lse = top + jnp.log(total)
    for n in range(q.shape[0] // 128):
        lse_ref[0, n : n + 1, :] = to_row(lse[n * 128 : (n + 1) * 128, :])


def batch_kernel(g_ref, q_ref, it_ref, sh_ref, out_ref, stat_ref, s_ref):
    peers = g_ref.shape[0]
    rows = q_ref.shape[0]
    keys = sh_ref.shape[1]
    q = q_ref[...]
    highest = None
    for k in range(peers):
        parts = g_ref[k, rows + keys :, 0:keys].astype(F32)
        shift = parts[0:1, :] + (parts[1:2, :] + parts[2:3, :])
        s = dot_rows(q, g_ref[k, rows : rows + keys, :]) + shift
        s_ref[k] = s
        highest = s if highest is None else jnp.maximum(highest, s)
    top = jnp.max(highest, axis=1, keepdims=True)
    total = jnp.zeros((rows, keys), F32)
    acc = jnp.zeros(q.shape, F32)
    for k in range(peers):
        p = jnp.exp(s_ref[k] - top)
        total = total + p
        acc = acc + dot_plain(p.astype(BF16), g_ref[k, rows : rows + keys, :])
    total = jnp.sum(total, axis=1, keepdims=True)
    out_ref[...] = acc / total
    stat_ref[0:1, :] = to_row(top + jnp.log(total))
    own = dot_rows(q, it_ref[...]) + sh_ref[:, 0:rows]
    stat_ref[1:2, :] = jnp.sum(jnp.where(eye(rows), own, 0.0), axis=0, keepdims=True)


def total_kernel(lse_ref, stat_ref, total_ref, loss_ref):
    lse = lse_ref[...]
    batch = stat_ref[0:1, :]
    top = jnp.maximum(jnp.max(lse, axis=0, keepdims=True), batch)
    summed = jnp.sum(jnp.exp(lse - top), axis=0, keepdims=True) + jnp.exp(batch - top)
    log_total = top + jnp.log(summed)
    total_ref[...] = log_total
    loss_ref[...] = log_total - stat_ref[1:2, :]


def item_kernel(g_ref, lt_ref, q_ref, it_ref, ng_ref, sh_ref, item_ref, neg_ref):
    peers = g_ref.shape[0]
    rows = q_ref.shape[0]
    items, negs = it_ref[...], ng_ref[...]
    shift_items = to_column(sh_ref[:, 0:rows])
    shift_negs = to_column(sh_ref[:, rows:])
    item_acc = jnp.zeros(items.shape, F32)
    neg_acc = jnp.zeros(negs.shape, F32)
    for k in range(peers):
        queries = g_ref[k, 0:rows, :]
        log_total = lt_ref[k : k + 1, :]
        w = jnp.exp(dot_rows(items, queries) + shift_items - log_total).astype(BF16)
        item_acc = item_acc + dot_plain(w, queries)
        w = jnp.exp(dot_rows(negs, queries) + shift_negs - log_total).astype(BF16)
        neg_acc = neg_acc + dot_plain(w, queries)
    item_ref[...] = item_acc - q_ref[...].astype(F32)
    neg_ref[...] = neg_acc


def query_kernel(parts_ref, lse_ref, lt_ref, batch_ref, stat_ref, it_ref, out_ref):
    log_total = lt_ref[...]
    out = batch_ref[...] * to_column(jnp.exp(stat_ref[0:1, :] - log_total))
    for k in range(parts_ref.shape[0]):
        share = to_column(jnp.exp(lse_ref[k : k + 1, :] - log_total))
        out = out + parts_ref[k].astype(F32) * share
    out_ref[...] = out - it_ref[...].astype(F32)


def local(
    query_vectors,
    item_vectors,
    negative_vectors,
    item_ids,
    negative_ids,
    negative_counts,
    memory,
    owners,
    memory_slots,
):
    rows, width = query_vectors.shape
    negatives = negative_vectors.shape[0]
    keys = rows + negatives
    mem = memory[0]
    half = mem.shape[0] // 2
    group = lax.axis_size("dp")
    shards = lax.axis_size("zh")
    depth = shards * lax.axis_size("zl")
    cycle = depth * lax.axis_size("yh")
    column = ("yh", "zh", "zl")

    def moved(block, over, by):
        route = [
            (y * depth + z, ((y + over) % 2) * depth + (z + by) % depth)
            for y in range(cycle // depth)
            for z in range(depth)
        ]
        return lax.ppermute(block, column, route)

    first, second = mem[:half], mem[half:]
    memory_blocks = [
        mem,
        moved(mem, 1, 0),
        moved(first, 0, -1),
        moved(second, 0, 1),
        moved(first, 1, -1),
        moved(second, 1, 1),
    ]
    column_queries = lax.all_gather(query_vectors, "zh", axis=0, tiled=True)

    batch_shift = -jnp.log(rows * group * sample_chance(item_ids))
    negative_shift = jnp.log(negative_counts.astype(F32)) - jnp.log(
        negatives * group * sample_chance(negative_ids)
    )
    shift = jnp.concatenate([batch_shift, negative_shift])[None, :]
    capacity = max(2, 2 * rows // cycle)
    block, outgoing = call(
        lambda *refs: prepare_kernel(capacity, *refs),
        (
            jax.ShapeDtypeStruct((rows + keys + 16, width), BF16),
            jax.ShapeDtypeStruct((cycle * capacity, width + 128), BF16),
        ),
        "prepare",
    )(
        query_vectors,
        item_vectors,
        negative_vectors,
        shift,
        owners,
        owners.reshape(1, rows),
        memory_slots.reshape(rows, 1),
    )
    gathered = lax.all_gather(block, "dp", axis=0, tiled=False)

    tile = 256
    count = column_queries.shape[0]
    total_rows = sum(b.shape[0] for b in memory_blocks)
    parts, lse = call(
        memory_kernel,
        (
            jax.ShapeDtypeStruct((count, width), BF16),
            jax.ShapeDtypeStruct((count // tile, tile // 128, 128), F32),
        ),
        "memory",
        grid=(count // tile,),
        in_specs=[pl.BlockSpec((tile, width), lambda i: (i, 0))]
        + [pl.BlockSpec(b.shape, lambda i: (0, 0)) for b in memory_blocks],
        out_specs=(
            pl.BlockSpec((tile, width), lambda i: (i, 0)),
            pl.BlockSpec((1, tile // 128, 128), lambda i: (i, 0, 0)),
        ),
        scratch_shapes=[pltpu.VMEM((tile, total_rows), F32)],
    )(column_queries, *memory_blocks)
    lse_back = lax.all_to_all(lse.reshape(shards, rows), "zh", 0, 0, tiled=True)
    parts, lse_back = lax.optimization_barrier((parts, lse_back))
    parts_back = lax.all_to_all(parts.reshape(shards, rows, width), "zh", 0, 0, tiled=True)

    batch_part, batch_stat = call(
        batch_kernel,
        (
            jax.ShapeDtypeStruct((rows, width), F32),
            jax.ShapeDtypeStruct((2, rows), F32),
        ),
        "batch",
        scratch_shapes=[pltpu.VMEM((group, rows, keys), F32)],
    )(gathered, query_vectors, item_vectors, shift)
    log_total, loss = call(
        total_kernel,
        (jax.ShapeDtypeStruct((1, rows), F32), jax.ShapeDtypeStruct((1, rows), F32)),
        "total",
    )(lse_back, batch_stat)
    group_totals = lax.all_gather(log_total, "dp", axis=0, tiled=True)
    item_grad, negative_grad = call(
        item_kernel,
        (
            jax.ShapeDtypeStruct((rows, width), F32),
            jax.ShapeDtypeStruct((negatives, width), F32),
        ),
        "items",
    )(gathered, group_totals, query_vectors, item_vectors, negative_vectors, shift)
    query_grad = call(query_kernel, jax.ShapeDtypeStruct((rows, width), F32), "queries")(
        parts_back, lse_back, log_total, batch_part, batch_stat, item_vectors
    )

    arrived = lax.all_to_all(outgoing, column, 0, 0, tiled=True)
    updated = call(update_kernel, jax.ShapeDtypeStruct(mem.shape, BF16), "update")(arrived, mem)
    return (loss[0], query_grad, item_grad, negative_grad, updated[None])


def solution(mesh):
    cycle, group = mesh.shape["mem"], mesh.shape["dp"]
    cut = Mesh(
        mesh.devices.reshape(2, cycle // 4, 2, group), ("yh", "zh", "zl", "dp")
    )
    spread = ("yh", "zh", "zl", "dp")
    column = ("yh", "zh", "zl")
    return jax.shard_map(
        local,
        mesh=cut,
        in_specs=(
            P(spread, None),
            P(spread, None),
            P(spread, None),
            P(spread),
            P(spread),
            P(spread),
            P("dp", column, None),
            P(spread, None),
            P(spread),
        ),
        out_specs=(
            P(spread),
            P(spread, None),
            P(spread, None),
            P(spread, None),
            P("dp", column, None),
        ),
        check_vma=False,
    )
```

```python
import math

import jax
import jax.numpy as jnp
from jax import lax
from jax.experimental import pallas as pl
from jax.experimental.pallas import tpu as pltpu
from jax.sharding import Mesh, PartitionSpec as P

ITEMS = 65536
BF16 = jnp.bfloat16
F32 = jnp.float32
VMEM_LIMIT = 56 * 1024 * 1024


def sample_chance(identities):
    return jnp.log1p(1.0 / (identities.astype(F32) + 1.0)) / math.log(ITEMS + 1)


def dot_rows(left, right):
    return lax.dot_general(left, right, (((1,), (1,)), ((), ())), preferred_element_type=F32)


def dot_plain(left, right):
    return jnp.dot(left, right, preferred_element_type=F32)


def eye(size):
    return lax.broadcasted_iota(jnp.int32, (size, size), 0) == lax.broadcasted_iota(
        jnp.int32, (size, size), 1
    )


def to_row(column):
    return jnp.sum(jnp.where(eye(column.shape[0]), column, 0), axis=0, keepdims=True)


def to_column(row):
    return jnp.sum(jnp.where(eye(row.shape[1]), row, 0), axis=1, keepdims=True)


def split_rows(row, count):
    high = row.astype(BF16).astype(F32)
    middle = (row - high).astype(BF16).astype(F32)
    low = row - high - middle
    place = lax.broadcasted_iota(jnp.int32, (count, row.shape[1]), 0)
    return jnp.where(
        place == 0, high, jnp.where(place == 1, middle, jnp.where(place == 2, low, 0.0))
    )


def joined(three):
    three = three.astype(F32)
    return three[0:1, :] + (three[1:2, :] + three[2:3, :])


def call(kernel, operands, out_shape, name, scratch=()):
    here = pl.BlockSpec(memory_space=pltpu.VMEM)
    return pl.pallas_call(
        kernel,
        out_shape=out_shape,
        in_specs=[here] * len(operands),
        out_specs=(here,) * len(out_shape),
        scratch_shapes=list(scratch),
        name=name,
        compiler_params=pltpu.CompilerParams(vmem_limit_bytes=VMEM_LIMIT),
    )(*operands)


def prepare_kernel(
    capacity,
    group,
    q_ref,
    it_ref,
    ng_ref,
    id_ref,
    ng_id_ref,
    ng_count_ref,
    owner_ref,
    slot_ref,
    block_ref,
    out_ref,
    sh_ref,
):
    rows, negs = q_ref.shape[0], ng_ref.shape[0]
    keys = rows + negs
    extra = block_ref.shape[0] - rows - keys
    sh_ref[:, 0:rows] = -jnp.log(rows * group * sample_chance(id_ref[...]))
    sh_ref[:, rows:] = jnp.log(ng_count_ref[...].astype(F32)) - jnp.log(
        negs * group * sample_chance(ng_id_ref[...])
    )
    block_ref[0:rows, :] = q_ref[...]
    block_ref[rows : 2 * rows, :] = it_ref[...]
    block_ref[2 * rows : rows + keys, :] = ng_ref[...]
    block_ref[rows + keys :, :] = jnp.zeros((extra, block_ref.shape[1]), BF16)
    block_ref[rows + keys :, 0:keys] = split_rows(sh_ref[...], extra).astype(BF16)

    count = it_ref.shape[0]
    own_row = owner_ref[...].astype(F32)
    own_col = to_column(own_row)
    earlier = lax.broadcasted_iota(jnp.int32, (count, count), 0) < lax.broadcasted_iota(
        jnp.int32, (count, count), 1
    )
    rank = jnp.sum(
        jnp.where(jnp.logical_and(own_col == own_row, earlier), 1.0, 0.0), axis=0, keepdims=True
    )
    target = (own_row * capacity + rank).astype(jnp.int32)
    places = out_ref.shape[0]
    chosen = jnp.where(
        lax.broadcasted_iota(jnp.int32, (places, count), 0) == target, 1.0, 0.0
    ).astype(BF16)
    slot = slot_ref[...]
    high = to_column((slot >> 5).astype(F32))
    low = to_column((slot & 31).astype(F32))
    lane = lax.broadcasted_iota(jnp.int32, (count, 128), 1)
    details = jnp.where(
        lane == 0, high, jnp.where(lane == 1, low, jnp.where(lane == 2, 1.0, 0.0))
    )
    width = it_ref.shape[1]
    out_ref[:, 0:width] = dot_plain(chosen, it_ref[...]).astype(BF16)
    out_ref[:, width:] = dot_plain(chosen, details.astype(BF16)).astype(BF16)


def update_kernel(got_ref, mem_ref, new_ref):
    places, width = got_ref.shape[0], mem_ref.shape[1]
    rows = mem_ref.shape[0]
    details = jnp.transpose(got_ref[:, width:].astype(F32))
    slot = details[0:1, :] * 32.0 + details[1:2, :]
    slot = jnp.where(details[2:3, :] > 0.5, slot, -1.0).astype(jnp.int32)
    entry = lax.broadcasted_iota(jnp.int32, (1, places), 1).astype(F32)
    step = 256
    for start in range(0, rows, step):
        row = lax.broadcasted_iota(jnp.int32, (step, places), 0) + start
        latest = jnp.max(jnp.where(row == slot, entry, -1.0), axis=1, keepdims=True)
        chosen = jnp.where(entry == latest, 1.0, 0.0).astype(BF16)
        fresh = dot_plain(chosen, got_ref[:, 0:width])
        old = mem_ref[start : start + step, :].astype(F32)
        new_ref[start : start + step, :] = jnp.where(latest >= 0.0, fresh, old).astype(BF16)


def memory_kernel(tile, *refs):
    q_ref, *mem_refs, out_ref = refs
    block = 128
    extra = out_ref.shape[1] - block
    step = 1024
    pieces, open_piece = [], []
    for ref in mem_refs:
        for at in range(0, ref.shape[0], step):
            open_piece.append(ref[at : at + step, :])
            if sum(p.shape[0] for p in open_piece) >= step:
                pieces.append(jnp.concatenate(open_piece, axis=0))
                open_piece = []

    def one_tile(n, carry):
        q = q_ref[pl.ds(pl.multiple_of(n * tile, tile), tile), :]
        top = jnp.full((tile, 1), -jnp.inf, F32)
        total = jnp.zeros((tile, 1), F32)
        acc = jnp.zeros(q.shape, F32)
        following = dot_rows(q, pieces[0])
        for k, rows in enumerate(pieces):
            s = following
            if k + 1 < len(pieces):
                following = dot_rows(q, pieces[k + 1])
            newest = jnp.maximum(top, jnp.max(s, axis=1, keepdims=True))
            p = jnp.exp(s - newest)
            scale = jnp.exp(top - newest)
            total = total * scale + jnp.sum(p, axis=1, keepdims=True)
            acc = acc * scale + dot_plain(p.astype(BF16), rows)
            top = newest
        average = (acc / total).astype(BF16)
        lse = top + jnp.log(total)
        for h in range(tile // block):
            at = n * (tile // block) + h
            out_ref[at, 0:block, :] = average[h * block : (h + 1) * block, :]
            lse_row = to_row(lse[h * block : (h + 1) * block, :])
            out_ref[at, block:, 0:block] = split_rows(lse_row, extra).astype(BF16)
            out_ref[at, block:, block:] = jnp.zeros((extra, q.shape[1] - block), BF16)
        return carry

    lax.fori_loop(0, q_ref.shape[0] // tile, one_tile, 0)


def batch_kernel(g_ref, q_ref, it_ref, sh_ref, out_ref, stat_ref, s_ref):
    peers = g_ref.shape[0]
    rows = q_ref.shape[0]
    keys = sh_ref.shape[1]
    q = q_ref[...]
    highest = None
    for k in range(peers):
        shift = joined(g_ref[k, rows + keys :, 0:keys])
        s = dot_rows(q, g_ref[k, rows : rows + keys, :]) + shift
        s_ref[k] = s
        highest = s if highest is None else jnp.maximum(highest, s)
    top = jnp.max(highest, axis=1, keepdims=True)
    total = jnp.zeros((rows, keys), F32)
    acc = jnp.zeros(q.shape, F32)
    for k in range(peers):
        p = jnp.exp(s_ref[k] - top)
        total = total + p
        acc = acc + dot_plain(p.astype(BF16), g_ref[k, rows : rows + keys, :])
    total = jnp.sum(total, axis=1, keepdims=True)
    out_ref[...] = acc / total
    stat_ref[0:1, :] = to_row(top + jnp.log(total))
    own = dot_rows(q, it_ref[...]) + sh_ref[:, 0:rows]
    stat_ref[1:2, :] = jnp.sum(jnp.where(eye(rows), own, 0.0), axis=0, keepdims=True)


def total_kernel(parts_ref, stat_ref, total_ref, loss_ref):
    rows = total_ref.shape[1]
    shards = parts_ref.shape[0]
    batch = stat_ref[0:1, :]
    lse = [joined(parts_ref[k, rows:, 0:rows]) for k in range(shards)]
    top = batch
    for row in lse:
        top = jnp.maximum(top, row)
    summed = jnp.exp(batch - top)
    for row in lse:
        summed = summed + jnp.exp(row - top)
    log_total = top + jnp.log(summed)
    total_ref[...] = log_total
    loss_ref[...] = log_total - stat_ref[1:2, :]


def item_kernel(g_ref, lt_ref, q_ref, it_ref, ng_ref, sh_ref, item_ref, neg_ref):
    peers = g_ref.shape[0]
    rows = q_ref.shape[0]
    items, negs = it_ref[...], ng_ref[...]
    shift_items = to_column(sh_ref[:, 0:rows])
    shift_negs = to_column(sh_ref[:, rows:])
    item_acc = jnp.zeros(items.shape, F32)
    neg_acc = jnp.zeros(negs.shape, F32)
    for k in range(peers):
        queries = g_ref[k, 0:rows, :]
        log_total = lt_ref[k : k + 1, :]
        w = jnp.exp(dot_rows(items, queries) + shift_items - log_total).astype(BF16)
        item_acc = item_acc + dot_plain(w, queries)
        w = jnp.exp(dot_rows(negs, queries) + shift_negs - log_total).astype(BF16)
        neg_acc = neg_acc + dot_plain(w, queries)
    item_ref[...] = item_acc - q_ref[...].astype(F32)
    neg_ref[...] = neg_acc


def query_kernel(parts_ref, lt_ref, batch_ref, stat_ref, it_ref, out_ref):
    log_total = lt_ref[...]
    rows = log_total.shape[1]
    out = batch_ref[...] * to_column(jnp.exp(stat_ref[0:1, :] - log_total))
    for k in range(parts_ref.shape[0]):
        share = to_column(jnp.exp(joined(parts_ref[k, rows:, 0:rows]) - log_total))
        out = out + parts_ref[k, 0:rows, :].astype(F32) * share
    out_ref[...] = out - it_ref[...].astype(F32)


def local(
    query_vectors,
    item_vectors,
    negative_vectors,
    item_ids,
    negative_ids,
    negative_counts,
    memory,
    owners,
    memory_slots,
):
    rows, width = query_vectors.shape
    negatives = negative_vectors.shape[0]
    keys = rows + negatives
    mem = memory[0]
    half = mem.shape[0] // 2
    group = lax.axis_size("dp")
    shards = lax.axis_size("zh")
    depth = shards * lax.axis_size("zl")
    cycle = depth * lax.axis_size("yh")
    column = ("yh", "zh", "zl")

    def moved(block, over, by):
        route = [
            (y * depth + z, ((y + over) % 2) * depth + (z + by) % depth)
            for y in range(cycle // depth)
            for z in range(depth)
        ]
        return lax.ppermute(block, column, route)

    def collected(block, axis):
        count = lax.axis_size(axis)
        return lax.all_to_all(
            jnp.broadcast_to(block[None], (count,) + block.shape), axis, 0, 0, tiled=True
        )

    column_queries = collected(query_vectors, "zh").reshape(-1, width)
    first, second = mem[:half], mem[half:]
    memory_blocks = [
        mem,
        moved(mem, 1, 0),
        moved(first, 0, -1),
        moved(second, 0, 1),
        moved(first, 1, -1),
        moved(second, 1, 1),
    ]

    capacity = max(2, 2 * rows // cycle)
    block, outgoing, shift = call(
        lambda *refs: prepare_kernel(capacity, group, *refs),
        (
            query_vectors,
            item_vectors,
            negative_vectors,
            item_ids[None, :],
            negative_ids[None, :],
            negative_counts[None, :],
            owners.reshape(1, rows),
            memory_slots[None, :],
        ),
        (
            jax.ShapeDtypeStruct((rows + keys + 16, width), BF16),
            jax.ShapeDtypeStruct((cycle * capacity, width + 128), BF16),
            jax.ShapeDtypeStruct((1, keys), F32),
        ),
        "prepare",
    )
    gathered = lax.all_gather(block, "dp", axis=0, tiled=False)

    column_queries, outgoing, *memory_blocks = lax.optimization_barrier(
        (column_queries, outgoing, *memory_blocks)
    )
    arrived = lax.all_to_all(
        outgoing.reshape(cycle, capacity, width + 128), column, 0, 0, tiled=True
    )
    (parts,) = call(
        lambda *refs: memory_kernel(512, *refs),
        (column_queries, *memory_blocks),
        (jax.ShapeDtypeStruct((shards, rows + 16, width), BF16),),
        "memory",
    )
    parts, arrived = lax.optimization_barrier((parts, arrived))
    parts_back = lax.all_to_all(parts, "zh", 0, 0, tiled=True)

    batch_part, batch_stat = call(
        batch_kernel,
        (gathered, query_vectors, item_vectors, shift),
        (
            jax.ShapeDtypeStruct((rows, width), F32),
            jax.ShapeDtypeStruct((2, rows), F32),
        ),
        "batch",
        [pltpu.VMEM((group, rows, keys), F32)],
    )
    (updated,) = call(
        update_kernel,
        (arrived.reshape(cycle * capacity, width + 128), mem),
        (jax.ShapeDtypeStruct(mem.shape, BF16),),
        "update",
    )
    parts_back, updated, batch_part, batch_stat = lax.optimization_barrier(
        (parts_back, updated, batch_part, batch_stat)
    )
    log_total, loss = call(
        total_kernel,
        (parts_back, batch_stat),
        (jax.ShapeDtypeStruct((1, rows), F32), jax.ShapeDtypeStruct((1, rows), F32)),
        "total",
    )
    group_totals = collected(log_total, "dp").reshape(group, rows)
    (query_grad,) = call(
        query_kernel,
        (parts_back, log_total, batch_part, batch_stat, item_vectors),
        (jax.ShapeDtypeStruct((rows, width), F32),),
        "queries",
    )
    group_totals, query_grad = lax.optimization_barrier((group_totals, query_grad))
    item_grad, negative_grad = call(
        item_kernel,
        (gathered, group_totals, query_vectors, item_vectors, negative_vectors, shift),
        (
            jax.ShapeDtypeStruct((rows, width), F32),
            jax.ShapeDtypeStruct((negatives, width), F32),
        ),
        "items",
    )
    return (loss[0], query_grad, item_grad, negative_grad, updated[None])


def solution(mesh):
    cycle, group = mesh.shape["mem"], mesh.shape["dp"]
    cut = Mesh(
        mesh.devices.reshape(2, cycle // 4, 2, group), ("yh", "zh", "zl", "dp")
    )
    spread = ("yh", "zh", "zl", "dp")
    column = ("yh", "zh", "zl")
    return jax.shard_map(
        local,
        mesh=cut,
        in_specs=(
            P(spread, None),
            P(spread, None),
            P(spread, None),
            P(spread),
            P(spread),
            P(spread),
            P("dp", column, None),
            P(spread, None),
            P(spread),
        ),
        out_specs=(
            P(spread),
            P(spread, None),
            P(spread, None),
            P(spread, None),
            P("dp", column, None),
        ),
        check_vma=False,
    )
```

```python
import math

import jax
import jax.numpy as jnp
from jax import lax
from jax.experimental import pallas as pl
from jax.experimental.pallas import tpu as pltpu
from jax.sharding import Mesh, PartitionSpec as P

ITEMS = 65536
BF16 = jnp.bfloat16
F32 = jnp.float32
VMEM_LIMIT = 56 * 1024 * 1024


def sample_chance(identities):
    return jnp.log1p(1.0 / (identities.astype(F32) + 1.0)) / math.log(ITEMS + 1)


def dot_rows(left, right):
    return lax.dot_general(left, right, (((1,), (1,)), ((), ())), preferred_element_type=F32)


def dot_plain(left, right):
    return jnp.dot(left, right, preferred_element_type=F32)


def eye(size):
    return lax.broadcasted_iota(jnp.int32, (size, size), 0) == lax.broadcasted_iota(
        jnp.int32, (size, size), 1
    )


def to_row(column):
    return jnp.sum(jnp.where(eye(column.shape[0]), column, 0), axis=0, keepdims=True)


def to_column(row):
    return jnp.sum(jnp.where(eye(row.shape[1]), row, 0), axis=1, keepdims=True)


def split_rows(row, count):
    high = row.astype(BF16).astype(F32)
    middle = (row - high).astype(BF16).astype(F32)
    low = row - high - middle
    place = lax.broadcasted_iota(jnp.int32, (count, row.shape[1]), 0)
    return jnp.where(
        place == 0, high, jnp.where(place == 1, middle, jnp.where(place == 2, low, 0.0))
    )


def joined(three):
    three = three.astype(F32)
    return three[0:1, :] + (three[1:2, :] + three[2:3, :])


def call(kernel, operands, out_shape, name, scratch=()):
    here = pl.BlockSpec(memory_space=pltpu.VMEM)
    scalars = pl.BlockSpec(memory_space=pltpu.SMEM)
    return pl.pallas_call(
        kernel,
        out_shape=out_shape,
        in_specs=[scalars if operand.shape == (3,) else here for operand in operands],
        out_specs=(here,) * len(out_shape),
        scratch_shapes=list(scratch),
        name=name,
        compiler_params=pltpu.CompilerParams(vmem_limit_bytes=VMEM_LIMIT),
    )(*operands)


def prepare_kernel(
    capacity,
    group,
    place_ref,
    q_ref,
    it_ref,
    ng_ref,
    id_ref,
    ng_id_ref,
    ng_count_ref,
    owner_ref,
    slot_ref,
    block_ref,
    out_ref,
    sh_ref,
):
    rows, negs = q_ref.shape[0], ng_ref.shape[0]
    keys = rows + negs
    extra = block_ref.shape[0] - rows - keys
    sh_ref[:, 0:rows] = -jnp.log(rows * group * sample_chance(id_ref[...]))
    sh_ref[:, rows:] = jnp.log(ng_count_ref[...].astype(F32)) - jnp.log(
        negs * group * sample_chance(ng_id_ref[...])
    )
    block_ref[0:rows, :] = q_ref[...]
    block_ref[rows : 2 * rows, :] = it_ref[...]
    block_ref[2 * rows : rows + keys, :] = ng_ref[...]
    block_ref[rows + keys :, :] = jnp.zeros((extra, block_ref.shape[1]), BF16)
    block_ref[rows + keys :, 0:keys] = split_rows(sh_ref[...], extra).astype(BF16)

    pairs = out_ref.shape[0]
    count = it_ref.shape[0]
    own_int = owner_ref[...]
    own_row = own_int.astype(F32)
    own_col = to_column(own_row)
    earlier = lax.broadcasted_iota(jnp.int32, (count, count), 0) < lax.broadcasted_iota(
        jnp.int32, (count, count), 1
    )
    rank = jnp.sum(
        jnp.where(jnp.logical_and(own_col == own_row, earlier), 1.0, 0.0), axis=0, keepdims=True
    ).astype(jnp.int32)
    half = own_int // (2 * pairs)
    depth = own_int - half * (2 * pairs)
    pair = depth // 2
    parity = depth - pair * 2
    other = jnp.where(half == place_ref[0], 0, 2) + jnp.where(parity == place_ref[1], 0, 1)
    target = (pair * 4 + other) * capacity + rank
    places = pairs * 4 * capacity
    chosen = jnp.where(
        lax.broadcasted_iota(jnp.int32, (places, count), 0) == target, 1.0, 0.0
    ).astype(BF16)
    slot = slot_ref[...]
    high = to_column((slot >> 5).astype(F32))
    low = to_column((slot & 31).astype(F32))
    lane = lax.broadcasted_iota(jnp.int32, (count, 128), 1)
    details = jnp.where(
        lane == 0, high, jnp.where(lane == 1, low, jnp.where(lane == 2, 1.0, 0.0))
    )
    sent = dot_plain(chosen, it_ref[...]).astype(BF16)
    sent_details = dot_plain(chosen, details.astype(BF16)).astype(BF16)
    span = 4 * capacity
    for k in range(pairs):
        out_ref[k, 0:rows, :] = q_ref[...]
        out_ref[k, rows : rows + span, :] = sent[k * span : (k + 1) * span, :]
        middle = k * span + span // 2
        out_ref[k, rows + span :, 0:128] = sent_details[k * span : middle, :]
        out_ref[k, rows + span :, 128:256] = sent_details[middle : (k + 1) * span, :]


def forward_kernel(rows, got_ref, *out_refs):
    pairs = got_ref.shape[0]
    span = (got_ref.shape[1] - rows) * 2 // 3
    each = span // 4
    width = got_ref.shape[2]
    for k in range(0, pairs, 2):
        items = [got_ref[k + n, rows : rows + span, :].astype(F32) for n in range(2)]
        details = [got_ref[k + n, rows + span :, :].astype(F32) for n in range(2)]
        for c, out_ref in enumerate(out_refs):
            at, side = (c % 2) * each, (c // 2) * 128
            out_ref[k * each : (k + 2) * each, 0:width] = jnp.concatenate(
                [block[c * each : (c + 1) * each, :] for block in items], axis=0
            ).astype(BF16)
            out_ref[k * each : (k + 2) * each, width:] = jnp.concatenate(
                [block[at : at + each, side : side + 128] for block in details], axis=0
            ).astype(BF16)


def update_kernel(pairs, place_ref, got0_ref, got1_ref, got2_ref, got3_ref, mem_ref, new_ref):
    rows, width = mem_ref.shape
    got = jnp.concatenate(
        [ref[...] for ref in (got0_ref, got1_ref, got2_ref, got3_ref)], axis=0
    )
    places = got.shape[0]
    each = places // (4 * pairs)
    details = jnp.transpose(got[:, width:].astype(F32))
    slot = details[0:1, :] * 32.0 + details[1:2, :]
    slot = jnp.where(details[2:3, :] > 0.5, slot, -1.0).astype(jnp.int32)
    entry = lax.broadcasted_iota(jnp.int32, (1, places), 1)
    other = entry // (pairs * each)
    inside = entry - other * (pairs * each)
    pair = inside // each
    rank = inside - pair * each
    flipped = other // 2
    half = jnp.where(flipped == 1, 1 - place_ref[0], place_ref[0])
    parity = jnp.where(other - 2 * flipped == 1, 1 - place_ref[1], place_ref[1])
    arrival = (((half * pairs + pair) * 2 + parity) * each + rank).astype(F32)
    items = got[:, 0:width]
    step = 256
    for start in range(0, rows, step):
        row = lax.broadcasted_iota(jnp.int32, (step, places), 0) + start
        latest = jnp.max(jnp.where(row == slot, arrival, -1.0), axis=1, keepdims=True)
        chosen = jnp.where(arrival == latest, 1.0, 0.0).astype(BF16)
        fresh = dot_plain(chosen, items)
        old = mem_ref[start : start + step, :].astype(F32)
        new_ref[start : start + step, :] = jnp.where(latest >= 0.0, fresh, old).astype(BF16)


def memory_kernel(tile, *refs):
    q_ref, *mem_refs, out_ref = refs
    block = 128
    extra = out_ref.shape[1] - block
    step = 1024
    pieces, open_piece = [], []
    for ref in mem_refs:
        for at in range(0, ref.shape[0], step):
            open_piece.append(ref[at : at + step, :])
            if sum(p.shape[0] for p in open_piece) >= step:
                pieces.append(jnp.concatenate(open_piece, axis=0))
                open_piece = []

    def one_tile(n, carry):
        q = jnp.concatenate(
            [q_ref[n * (tile // block) + h, 0:block, :] for h in range(tile // block)], axis=0
        )
        top = jnp.full((tile, 1), -jnp.inf, F32)
        total = jnp.zeros((tile, 1), F32)
        acc = jnp.zeros(q.shape, F32)
        following = dot_rows(q, pieces[0])
        for k, rows in enumerate(pieces):
            s = following
            if k + 1 < len(pieces):
                following = dot_rows(q, pieces[k + 1])
            newest = jnp.maximum(top, jnp.max(s, axis=1, keepdims=True))
            p = jnp.exp(s - newest)
            scale = jnp.exp(top - newest)
            total = total * scale + jnp.sum(p, axis=1, keepdims=True)
            acc = acc * scale + dot_plain(p.astype(BF16), rows)
            top = newest
        average = (acc / total).astype(BF16)
        lse = top + jnp.log(total)
        for h in range(tile // block):
            at = n * (tile // block) + h
            out_ref[at, 0:block, :] = average[h * block : (h + 1) * block, :]
            lse_row = to_row(lse[h * block : (h + 1) * block, :])
            out_ref[at, block:, 0:block] = split_rows(lse_row, extra).astype(BF16)
            out_ref[at, block:, block:] = jnp.zeros((extra, q.shape[1] - block), BF16)
        return carry

    lax.fori_loop(0, q_ref.shape[0] * block // tile, one_tile, 0)


def batch_kernel(*refs):
    *g_refs, q_ref, it_ref, sh_ref, out_ref, stat_ref, s_ref = refs
    rows = q_ref.shape[0]
    keys = sh_ref.shape[1]
    blocks = [(ref, k) for ref in g_refs for k in range(ref.shape[0])]
    q = q_ref[...]
    highest = None
    for n, (ref, k) in enumerate(blocks):
        shift = joined(ref[k, rows + keys :, 0:keys])
        s = dot_rows(q, ref[k, rows : rows + keys, :]) + shift
        s_ref[n] = s
        highest = s if highest is None else jnp.maximum(highest, s)
    top = jnp.max(highest, axis=1, keepdims=True)
    total = jnp.zeros((rows, keys), F32)
    acc = jnp.zeros(q.shape, F32)
    for n, (ref, k) in enumerate(blocks):
        p = jnp.exp(s_ref[n] - top)
        total = total + p
        acc = acc + dot_plain(p.astype(BF16), ref[k, rows : rows + keys, :])
    total = jnp.sum(total, axis=1, keepdims=True)
    out_ref[...] = acc / total
    stat_ref[0:1, :] = to_row(top + jnp.log(total))
    own = dot_rows(q, it_ref[...]) + sh_ref[:, 0:rows]
    stat_ref[1:2, :] = jnp.sum(jnp.where(eye(rows), own, 0.0), axis=0, keepdims=True)


def total_kernel(parts_ref, stat_ref, total_ref, loss_ref):
    rows = total_ref.shape[1]
    shards = parts_ref.shape[0]
    batch = stat_ref[0:1, :]
    lse = [joined(parts_ref[k, rows:, 0:rows]) for k in range(shards)]
    top = batch
    for row in lse:
        top = jnp.maximum(top, row)
    summed = jnp.exp(batch - top)
    for row in lse:
        summed = summed + jnp.exp(row - top)
    log_total = top + jnp.log(summed)
    total_ref[...] = log_total
    loss_ref[...] = log_total - stat_ref[1:2, :]


def item_kernel(*refs):
    place_ref, *g_refs, lt_ref, q_ref, it_ref, ng_ref, sh_ref, item_ref, neg_ref = refs
    rows = q_ref.shape[0]
    here = place_ref[2]
    near = g_refs[0].shape[0]
    peers = sum(ref.shape[0] for ref in g_refs)
    keys = jnp.concatenate([it_ref[...], ng_ref[...]], axis=0)
    shift = to_column(sh_ref[...])
    acc = jnp.zeros(keys.shape, F32)
    low = lax.rem(here, near)
    blocks = [(ref, k) for ref in g_refs for k in range(ref.shape[0])]
    for at in range(0, peers, 2):
        base = lax.rem(here - low - (at // near) * near + peers, peers)
        pair = blocks[at : at + 2]
        queries = jnp.concatenate([ref[k, 0:rows, :] for ref, k in pair], axis=0)
        log_total = jnp.concatenate(
            [lt_ref[pl.ds(base + (low ^ ((at + n) % near)), 1), :] for n in range(2)], axis=1
        )
        w = jnp.exp(dot_rows(keys, queries) + shift - log_total).astype(BF16)
        acc = acc + dot_plain(w, queries)
    item_ref[...] = acc[0:rows, :] - q_ref[...].astype(F32)
    neg_ref[...] = acc[rows:, :]


def query_kernel(parts_ref, lt_ref, batch_ref, stat_ref, it_ref, out_ref):
    log_total = lt_ref[...]
    rows = log_total.shape[1]
    out = batch_ref[...] * to_column(jnp.exp(stat_ref[0:1, :] - log_total))
    for k in range(parts_ref.shape[0]):
        share = to_column(jnp.exp(joined(parts_ref[k, rows:, 0:rows]) - log_total))
        out = out + parts_ref[k, 0:rows, :].astype(F32) * share
    out_ref[...] = out - it_ref[...].astype(F32)


def local(
    query_vectors,
    item_vectors,
    negative_vectors,
    item_ids,
    negative_ids,
    negative_counts,
    memory,
    owners,
    memory_slots,
):
    rows, width = query_vectors.shape
    negatives = negative_vectors.shape[0]
    keys = rows + negatives
    mem = memory[0]
    group = lax.axis_size("dp")
    shards = lax.axis_size("zh")
    depth = shards * lax.axis_size("zl")
    cycle = depth * lax.axis_size("yh")
    column = ("yh", "zh", "zl")

    def beside(block, over, by):
        route = [
            (y * depth + z, ((y + over) % 2) * depth + (z ^ by))
            for y in range(cycle // depth)
            for z in range(depth)
        ]
        return lax.ppermute(block, column, route)

    place = jnp.stack([lax.axis_index("yh"), lax.axis_index("zl"), lax.axis_index("dp")])
    capacity = max(2, 2 * rows // cycle)
    span = 4 * capacity
    block, outgoing, shift = call(
        lambda *refs: prepare_kernel(capacity, group, *refs),
        (
            place,
            query_vectors,
            item_vectors,
            negative_vectors,
            item_ids[None, :],
            negative_ids[None, :],
            negative_counts[None, :],
            owners.reshape(1, rows),
            memory_slots[None, :],
        ),
        (
            jax.ShapeDtypeStruct((rows + keys + 16, width), BF16),
            jax.ShapeDtypeStruct((shards, rows + span + span // 2, width), BF16),
            jax.ShapeDtypeStruct((1, keys), F32),
        ),
        "prepare",
    )
    arrived = lax.all_to_all(outgoing, "zh", 0, 0, tiled=True)

    near = 4
    pair_blocks = jnp.stack(
        [block] + [lax.ppermute(block, "dp", [(i, i ^ k) for i in range(group)]) for k in range(1, near)]
    )
    z_rows = beside(mem, 0, 1)
    memory_blocks = [mem, z_rows, beside(mem, 1, 0), beside(z_rows, 1, 0)]

    def along(blocks, by):
        return lax.ppermute(blocks, "dp", [(i, (i + near * by) % group) for i in range(group)])

    before, after = along(pair_blocks, 1), along(pair_blocks, -1)
    arrived, before, after, *memory_blocks = lax.optimization_barrier(
        (arrived, before, after, *memory_blocks)
    )

    (parts,) = call(
        lambda *refs: memory_kernel(512, *refs),
        (arrived, *memory_blocks),
        (jax.ShapeDtypeStruct((shards, rows + 16, width), BF16),),
        "memory",
    )
    parts, arrived, before, after = lax.optimization_barrier((parts, arrived, before, after))
    parts_back = lax.all_to_all(parts, "zh", 0, 0, tiled=True)

    group_blocks = [
        pair_blocks,
        before,
        along(before[: near // 2], 1),
        along(after[near // 2 :], -1),
        after,
    ]
    own_items, *others_items = call(
        lambda *refs: forward_kernel(rows, *refs),
        (arrived,),
        (jax.ShapeDtypeStruct((shards * capacity, width + 128), BF16),) * 4,
        "forward",
    )
    new_items = [own_items] + [
        beside(items, c // 2, c % 2) for c, items in enumerate(others_items, start=1)
    ]
    batch_part, batch_stat = call(
        batch_kernel,
        (*group_blocks, query_vectors, item_vectors, shift),
        (
            jax.ShapeDtypeStruct((rows, width), F32),
            jax.ShapeDtypeStruct((2, rows), F32),
        ),
        "batch",
        [pltpu.VMEM((group, rows, keys), F32)],
    )
    parts_back, batch_part, batch_stat, *new_items = lax.optimization_barrier(
        (parts_back, batch_part, batch_stat, *new_items)
    )
    log_total, loss = call(
        total_kernel,
        (parts_back, batch_stat),
        (jax.ShapeDtypeStruct((1, rows), F32), jax.ShapeDtypeStruct((1, rows), F32)),
        "total",
    )
    group_totals = lax.all_to_all(
        jnp.broadcast_to(log_total[None], (group, 1, rows)), "dp", 0, 0, tiled=True
    ).reshape(group, rows)
    (query_grad,) = call(
        query_kernel,
        (parts_back, log_total, batch_part, batch_stat, item_vectors),
        (jax.ShapeDtypeStruct((rows, width), F32),),
        "queries",
    )
    (updated,) = call(
        lambda *refs: update_kernel(shards, *refs),
        (place, *new_items, mem),
        (jax.ShapeDtypeStruct(mem.shape, BF16),),
        "update",
    )
    group_totals, query_grad, updated = lax.optimization_barrier(
        (group_totals, query_grad, updated)
    )
    item_grad, negative_grad = call(
        item_kernel,
        (
            place,
            *group_blocks,
            group_totals,
            query_vectors,
            item_vectors,
            negative_vectors,
            shift,
        ),
        (
            jax.ShapeDtypeStruct((rows, width), F32),
            jax.ShapeDtypeStruct((negatives, width), F32),
        ),
        "items",
    )
    return (loss[0], query_grad, item_grad, negative_grad, updated[None])


def solution(mesh):
    cycle, group = mesh.shape["mem"], mesh.shape["dp"]
    cut = Mesh(
        mesh.devices.reshape(2, cycle // 4, 2, group), ("yh", "zh", "zl", "dp")
    )
    spread = ("yh", "zh", "zl", "dp")
    column = ("yh", "zh", "zl")
    return jax.shard_map(
        local,
        mesh=cut,
        in_specs=(
            P(spread, None),
            P(spread, None),
            P(spread, None),
            P(spread),
            P(spread),
            P(spread),
            P("dp", column, None),
            P(spread, None),
            P(spread),
        ),
        out_specs=(
            P(spread),
            P(spread, None),
            P(spread, None),
            P(spread, None),
            P("dp", column, None),
        ),
        check_vma=False,
    )
```

```python
import math

import jax
import jax.numpy as jnp
from jax import lax
from jax.experimental import pallas as pl
from jax.experimental.pallas import tpu as pltpu
from jax.sharding import Mesh, PartitionSpec as P

ITEMS = 65536
BF16 = jnp.bfloat16
F32 = jnp.float32
VMEM_LIMIT = 56 * 1024 * 1024


def sample_chance(identities):
    return jnp.log1p(1.0 / (identities.astype(F32) + 1.0)) / math.log(ITEMS + 1)


def dot_rows(left, right):
    return lax.dot_general(left, right, (((1,), (1,)), ((), ())), preferred_element_type=F32)


def dot_plain(left, right):
    return jnp.dot(left, right, preferred_element_type=F32)


def eye(size):
    return lax.broadcasted_iota(jnp.int32, (size, size), 0) == lax.broadcasted_iota(
        jnp.int32, (size, size), 1
    )


def to_row(column):
    return jnp.sum(jnp.where(eye(column.shape[0]), column, 0), axis=0, keepdims=True)


def to_column(row):
    return jnp.sum(jnp.where(eye(row.shape[1]), row, 0), axis=1, keepdims=True)


def split_rows(row, count):
    high = row.astype(BF16).astype(F32)
    middle = (row - high).astype(BF16).astype(F32)
    low = row - high - middle
    place = lax.broadcasted_iota(jnp.int32, (count, row.shape[1]), 0)
    return jnp.where(
        place == 0, high, jnp.where(place == 1, middle, jnp.where(place == 2, low, 0.0))
    )


def joined(three):
    three = three.astype(F32)
    return three[0:1, :] + (three[1:2, :] + three[2:3, :])


def call(kernel, operands, out_shape, name, scratch=()):
    here = pl.BlockSpec(memory_space=pltpu.VMEM)
    scalars = pl.BlockSpec(memory_space=pltpu.SMEM)
    return pl.pallas_call(
        kernel,
        out_shape=out_shape,
        in_specs=[scalars if operand.shape == (3,) else here for operand in operands],
        out_specs=(here,) * len(out_shape),
        scratch_shapes=list(scratch),
        name=name,
        compiler_params=pltpu.CompilerParams(vmem_limit_bytes=VMEM_LIMIT),
    )(*operands)


def prepare_kernel(
    capacity,
    group,
    place_ref,
    q_ref,
    it_ref,
    ng_ref,
    id_ref,
    ng_id_ref,
    ng_count_ref,
    owner_ref,
    slot_ref,
    block_ref,
    copies_ref,
    sh_ref,
    *out_refs,
):
    rows, negs = q_ref.shape[0], ng_ref.shape[0]
    keys = rows + negs
    extra = block_ref.shape[0] - rows - keys
    sh_ref[:, 0:rows] = -jnp.log(rows * group * sample_chance(id_ref[...]))
    sh_ref[:, rows:] = jnp.log(ng_count_ref[...].astype(F32)) - jnp.log(
        negs * group * sample_chance(ng_id_ref[...])
    )
    block_ref[0:rows, :] = q_ref[...]
    block_ref[rows : 2 * rows, :] = it_ref[...]
    block_ref[2 * rows : rows + keys, :] = ng_ref[...]
    block_ref[rows + keys :, :] = jnp.zeros((extra, block_ref.shape[1]), BF16)
    block_ref[rows + keys :, 0:keys] = split_rows(sh_ref[...], extra).astype(BF16)

    pairs = copies_ref.shape[0]
    for k in range(pairs):
        copies_ref[k] = q_ref[...]
    count = it_ref.shape[0]
    own_int = owner_ref[...]
    own_row = own_int.astype(F32)
    own_col = to_column(own_row)
    earlier = lax.broadcasted_iota(jnp.int32, (count, count), 0) < lax.broadcasted_iota(
        jnp.int32, (count, count), 1
    )
    rank = jnp.sum(
        jnp.where(jnp.logical_and(own_col == own_row, earlier), 1.0, 0.0), axis=0, keepdims=True
    ).astype(jnp.int32)
    half = own_int // (2 * pairs)
    depth = own_int - half * (2 * pairs)
    pair = depth // 2
    parity = depth - pair * 2
    other = jnp.where(half == place_ref[0], 0, 2) + jnp.where(parity == place_ref[1], 0, 1)
    target = (other * pairs + pair) * capacity + rank
    places = pairs * 4 * capacity
    chosen = jnp.where(
        lax.broadcasted_iota(jnp.int32, (places, count), 0) == target, 1.0, 0.0
    ).astype(BF16)
    slot = slot_ref[...]
    high = to_column((slot >> 5).astype(F32))
    low = to_column((slot & 31).astype(F32))
    lane = lax.broadcasted_iota(jnp.int32, (count, 128), 1).astype(F32)
    lane = lane - 8.0 * to_column((other // 2).astype(F32))
    details = jnp.where(
        lane == 0.0, high, jnp.where(lane == 1.0, low, jnp.where(lane == 2.0, 1.0, 0.0))
    )
    width = it_ref.shape[1]
    each = places // 4
    for c, out_ref in enumerate(out_refs):
        some = chosen[c * each : (c + 1) * each, :]
        out_ref[:, 0:width] = dot_plain(some, it_ref[...]).astype(BF16)
        out_ref[:, width:] = dot_plain(some, details.astype(BF16)).astype(BF16)


def update_kernel(block, each, place_ref, got_ref, mem_ref, new_ref):
    rows, width = mem_ref.shape
    pairs = got_ref.shape[0]
    two = 2 * each
    items = jnp.concatenate(
        [
            got_ref[k, block + (1 + n) * two : block + (2 + n) * two, :]
            for n in range(2)
            for k in range(pairs)
        ],
        axis=0,
    )
    details = jnp.transpose(
        jnp.concatenate(
            [got_ref[k, block : block + two, block:].astype(F32) for k in range(pairs)], axis=0
        )
    )
    high, low, valid = (
        jnp.concatenate([details[n : n + 1, :], details[8 + n : 9 + n, :]], axis=1)
        for n in range(3)
    )
    slot = jnp.where(valid > 0.5, high * 32.0 + low, -1.0).astype(jnp.int32)
    places = items.shape[0]
    entry = lax.broadcasted_iota(jnp.int32, (1, places), 1)
    flipped = entry // (pairs * two)
    inside = entry - flipped * (pairs * two)
    pair = inside // two
    inside = inside - pair * two
    crossed = inside // each
    rank = inside - crossed * each
    half = jnp.where(flipped == 1, 1 - place_ref[0], place_ref[0])
    parity = jnp.where(crossed == 1, 1 - place_ref[1], place_ref[1])
    arrival = (((half * pairs + pair) * 2 + parity) * each + rank).astype(F32)
    step = 256
    for start in range(0, rows, step):
        row = lax.broadcasted_iota(jnp.int32, (step, places), 0) + start
        latest = jnp.max(jnp.where(row == slot, arrival, -1.0), axis=1, keepdims=True)
        chosen = jnp.where(arrival == latest, 1.0, 0.0).astype(BF16)
        fresh = dot_plain(chosen, items)
        old = mem_ref[start : start + step, :].astype(F32)
        new_ref[start : start + step, :] = jnp.where(latest >= 0.0, fresh, old).astype(BF16)


def memory_kernel(tile, *refs):
    q_ref, *mem_refs, item0_ref, item1_ref, item2_ref, item3_ref, out_ref = refs
    pairs, block, width = q_ref.shape
    each = item0_ref.shape[0] // pairs
    extra = 2 * each
    for k in range(0, pairs, 2):
        group = [
            ref[k * each : (k + 2) * each, :].astype(F32)
            for ref in (item0_ref, item1_ref, item2_ref, item3_ref)
        ]
        for n in range(2):
            one = [rows[n * each : (n + 1) * each, :] for rows in group]
            near = jnp.concatenate(one[0:2], axis=0)
            far = jnp.concatenate(one[2:4], axis=0)
            out_ref[k + n, block + extra : block + 2 * extra, :] = near[:, 0:width].astype(BF16)
            out_ref[k + n, block + 2 * extra :, :] = far[:, 0:width].astype(BF16)
            out_ref[k + n, block : block + extra, block:] = (
                near[:, width:] + far[:, width:]
            ).astype(BF16)
    step = 1024
    pieces, open_piece = [], []
    for ref in mem_refs:
        for at in range(0, ref.shape[0], step):
            open_piece.append(ref[at : at + step, :])
            if sum(p.shape[0] for p in open_piece) >= step:
                pieces.append(jnp.concatenate(open_piece, axis=0))
                open_piece = []

    def one_tile(n, carry):
        q = jnp.concatenate(
            [q_ref[n * (tile // block) + h, 0:block, :] for h in range(tile // block)], axis=0
        )
        top = jnp.full((tile, 1), -jnp.inf, F32)
        total = jnp.zeros((tile, 1), F32)
        acc = jnp.zeros(q.shape, F32)
        following = dot_rows(q, pieces[0])
        for k, rows in enumerate(pieces):
            s = following
            if k + 1 < len(pieces):
                following = dot_rows(q, pieces[k + 1])
            newest = jnp.maximum(top, jnp.max(s, axis=1, keepdims=True))
            p = jnp.exp(s - newest)
            scale = jnp.exp(top - newest)
            total = total * scale + jnp.sum(p, axis=1, keepdims=True)
            acc = acc * scale + dot_plain(p.astype(BF16), rows)
            top = newest
        average = (acc / total).astype(BF16)
        lse = top + jnp.log(total)
        for h in range(tile // block):
            at = n * (tile // block) + h
            out_ref[at, 0:block, :] = average[h * block : (h + 1) * block, :]
            lse_row = to_row(lse[h * block : (h + 1) * block, :])
            out_ref[at, block : block + extra, 0:block] = split_rows(lse_row, extra).astype(BF16)
        return carry

    lax.fori_loop(0, q_ref.shape[0] * block // tile, one_tile, 0)


def batch_kernel(*refs):
    *g_refs, q_ref, it_ref, sh_ref, out_ref, stat_ref, s_ref = refs
    rows = q_ref.shape[0]
    keys = sh_ref.shape[1]
    blocks = [(ref, k) for ref in g_refs for k in range(ref.shape[0])]
    q = q_ref[...]
    highest = None
    for n, (ref, k) in enumerate(blocks):
        shift = joined(ref[k, rows + keys :, 0:keys])
        s = dot_rows(q, ref[k, rows : rows + keys, :]) + shift
        s_ref[n] = s
        highest = s if highest is None else jnp.maximum(highest, s)
    top = jnp.max(highest, axis=1, keepdims=True)
    total = jnp.zeros((rows, keys), F32)
    acc = jnp.zeros(q.shape, F32)
    for n, (ref, k) in enumerate(blocks):
        p = jnp.exp(s_ref[n] - top)
        total = total + p
        acc = acc + dot_plain(p.astype(BF16), ref[k, rows : rows + keys, :])
    total = jnp.sum(total, axis=1, keepdims=True)
    out_ref[...] = acc / total
    stat_ref[0:1, :] = to_row(top + jnp.log(total))
    own = dot_rows(q, it_ref[...]) + sh_ref[:, 0:rows]
    stat_ref[1:2, :] = jnp.sum(jnp.where(eye(rows), own, 0.0), axis=0, keepdims=True)


def total_kernel(parts_ref, stat_ref, total_ref, loss_ref):
    rows = total_ref.shape[1]
    shards = parts_ref.shape[0]
    batch = stat_ref[0:1, :]
    lse = [joined(parts_ref[k, rows : rows + 16, 0:rows]) for k in range(shards)]
    top = batch
    for row in lse:
        top = jnp.maximum(top, row)
    summed = jnp.exp(batch - top)
    for row in lse:
        summed = summed + jnp.exp(row - top)
    log_total = top + jnp.log(summed)
    total_ref[...] = log_total
    loss_ref[...] = log_total - stat_ref[1:2, :]


def item_kernel(*refs):
    place_ref, *g_refs, lt_ref, q_ref, it_ref, ng_ref, sh_ref, item_ref, neg_ref = refs
    rows = q_ref.shape[0]
    here = place_ref[2]
    near = g_refs[0].shape[0]
    peers = sum(ref.shape[0] for ref in g_refs)
    keys = jnp.concatenate([it_ref[...], ng_ref[...]], axis=0)
    shift = to_column(sh_ref[...])
    acc = jnp.zeros(keys.shape, F32)
    low = lax.rem(here, near)
    blocks = [(ref, k) for ref in g_refs for k in range(ref.shape[0])]
    for at in range(0, peers, 2):
        base = lax.rem(here - low - (at // near) * near + peers, peers)
        pair = blocks[at : at + 2]
        queries = jnp.concatenate([ref[k, 0:rows, :] for ref, k in pair], axis=0)
        log_total = jnp.concatenate(
            [lt_ref[pl.ds(base + (low ^ ((at + n) % near)), 1), :] for n in range(2)], axis=1
        )
        w = jnp.exp(dot_rows(keys, queries) + shift - log_total).astype(BF16)
        acc = acc + dot_plain(w, queries)
    item_ref[...] = acc[0:rows, :] - q_ref[...].astype(F32)
    neg_ref[...] = acc[rows:, :]


def query_kernel(parts_ref, lt_ref, batch_ref, stat_ref, it_ref, out_ref):
    log_total = lt_ref[...]
    rows = log_total.shape[1]
    out = batch_ref[...] * to_column(jnp.exp(stat_ref[0:1, :] - log_total))
    for k in range(parts_ref.shape[0]):
        share = to_column(jnp.exp(joined(parts_ref[k, rows : rows + 16, 0:rows]) - log_total))
        out = out + parts_ref[k, 0:rows, :].astype(F32) * share
    out_ref[...] = out - it_ref[...].astype(F32)


def local(
    query_vectors,
    item_vectors,
    negative_vectors,
    item_ids,
    negative_ids,
    negative_counts,
    memory,
    owners,
    memory_slots,
):
    rows, width = query_vectors.shape
    negatives = negative_vectors.shape[0]
    keys = rows + negatives
    mem = memory[0]
    group = lax.axis_size("dp")
    shards = lax.axis_size("zh")
    depth = shards * lax.axis_size("zl")
    cycle = depth * lax.axis_size("yh")
    column = ("yh", "zh", "zl")

    def beside(block, over, by):
        route = [
            (y * depth + z, ((y + over) % 2) * depth + (z ^ by))
            for y in range(cycle // depth)
            for z in range(depth)
        ]
        return lax.ppermute(block, column, route)

    place = jnp.stack([lax.axis_index("yh"), lax.axis_index("zl"), lax.axis_index("dp")])
    capacity = max(2, 2 * rows // cycle)
    block, copies, shift, *new_items = call(
        lambda *refs: prepare_kernel(capacity, group, *refs),
        (
            place,
            query_vectors,
            item_vectors,
            negative_vectors,
            item_ids[None, :],
            negative_ids[None, :],
            negative_counts[None, :],
            owners.reshape(1, rows),
            memory_slots[None, :],
        ),
        (
            jax.ShapeDtypeStruct((rows + keys + 16, width), BF16),
            jax.ShapeDtypeStruct((shards, rows, width), BF16),
            jax.ShapeDtypeStruct((1, keys), F32),
        )
        + (jax.ShapeDtypeStruct((shards * capacity, width + 128), BF16),) * 4,
        "prepare",
    )
    new_items = [new_items[0]] + [beside(new_items[c], c // 2, c % 2) for c in range(1, 4)]

    near = 4
    near_blocks = [block] + [
        lax.ppermute(block, "dp", [(i, i ^ k) for i in range(group)]) for k in range(1, near)
    ]
    pair_blocks = jnp.stack(near_blocks)
    z_rows = beside(mem, 0, 1)
    copies, z_rows, pair_blocks = lax.optimization_barrier((copies, z_rows, pair_blocks))
    arrived = lax.all_to_all(copies, "zh", 0, 0, tiled=True)
    memory_blocks = [mem, z_rows, beside(mem, 1, 0), beside(z_rows, 1, 0)]

    def along(blocks, by):
        return lax.ppermute(blocks, "dp", [(i, (i + near * by) % group) for i in range(group)])

    before, after = along(pair_blocks, 1), along(pair_blocks, -1)
    arrived, before, after, memory_blocks = lax.optimization_barrier(
        (arrived, before, after, memory_blocks)
    )

    (parts,) = call(
        lambda *refs: memory_kernel(512, *refs),
        (arrived, *memory_blocks, *new_items),
        (jax.ShapeDtypeStruct((shards, rows + 6 * capacity, width), BF16),),
        "memory",
    )
    parts, before, after = lax.optimization_barrier((parts, before, after))
    parts_back = lax.all_to_all(parts, "zh", 0, 0, tiled=True)

    group_blocks = [
        pair_blocks,
        before,
        along(before[: near // 2], 1),
        along(after[near // 2 :], -1),
        after,
    ]
    batch_part, batch_stat = call(
        batch_kernel,
        (*group_blocks, query_vectors, item_vectors, shift),
        (
            jax.ShapeDtypeStruct((rows, width), F32),
            jax.ShapeDtypeStruct((2, rows), F32),
        ),
        "batch",
        [pltpu.VMEM((group, rows, keys), F32)],
    )
    parts_back, batch_part, batch_stat = lax.optimization_barrier(
        (parts_back, batch_part, batch_stat)
    )
    log_total, loss = call(
        total_kernel,
        (parts_back, batch_stat),
        (jax.ShapeDtypeStruct((1, rows), F32), jax.ShapeDtypeStruct((1, rows), F32)),
        "total",
    )
    group_totals = lax.all_to_all(
        jnp.broadcast_to(log_total[None], (group, 1, rows)), "dp", 0, 0, tiled=True
    ).reshape(group, rows)
    (query_grad,) = call(
        query_kernel,
        (parts_back, log_total, batch_part, batch_stat, item_vectors),
        (jax.ShapeDtypeStruct((rows, width), F32),),
        "queries",
    )
    (updated,) = call(
        lambda *refs: update_kernel(rows, capacity, *refs),
        (place, parts_back, mem),
        (jax.ShapeDtypeStruct(mem.shape, BF16),),
        "update",
    )
    group_totals, query_grad, updated = lax.optimization_barrier(
        (group_totals, query_grad, updated)
    )
    item_grad, negative_grad = call(
        item_kernel,
        (
            place,
            *group_blocks,
            group_totals,
            query_vectors,
            item_vectors,
            negative_vectors,
            shift,
        ),
        (
            jax.ShapeDtypeStruct((rows, width), F32),
            jax.ShapeDtypeStruct((negatives, width), F32),
        ),
        "items",
    )
    return (loss[0], query_grad, item_grad, negative_grad, updated[None])


def solution(mesh):
    cycle, group = mesh.shape["mem"], mesh.shape["dp"]
    cut = Mesh(
        mesh.devices.reshape(2, cycle // 4, 2, group), ("yh", "zh", "zl", "dp")
    )
    spread = ("yh", "zh", "zl", "dp")
    column = ("yh", "zh", "zl")
    return jax.shard_map(
        local,
        mesh=cut,
        in_specs=(
            P(spread, None),
            P(spread, None),
            P(spread, None),
            P(spread),
            P(spread),
            P(spread),
            P("dp", column, None),
            P(spread, None),
            P(spread),
        ),
        out_specs=(
            P(spread),
            P(spread, None),
            P(spread, None),
            P(spread, None),
            P("dp", column, None),
        ),
        check_vma=False,
    )
```

```python
import math

import jax
import jax.numpy as jnp
from jax import lax
from jax.experimental import pallas as pl
from jax.experimental.pallas import tpu as pltpu
from jax.sharding import Mesh, PartitionSpec as P

ITEMS = 65536
BF16 = jnp.bfloat16
F32 = jnp.float32
VMEM_LIMIT = 56 * 1024 * 1024


def sample_chance(identities):
    return jnp.log1p(1.0 / (identities.astype(F32) + 1.0)) / math.log(ITEMS + 1)


def dot_rows(left, right):
    return lax.dot_general(left, right, (((1,), (1,)), ((), ())), preferred_element_type=F32)


def dot_plain(left, right):
    return jnp.dot(left, right, preferred_element_type=F32)


def eye(size):
    return lax.broadcasted_iota(jnp.int32, (size, size), 0) == lax.broadcasted_iota(
        jnp.int32, (size, size), 1
    )


def to_row(column):
    return jnp.sum(jnp.where(eye(column.shape[0]), column, 0), axis=0, keepdims=True)


def to_column(row):
    return jnp.sum(jnp.where(eye(row.shape[1]), row, 0), axis=1, keepdims=True)


def split_rows(row, count):
    high = row.astype(BF16).astype(F32)
    middle = (row - high).astype(BF16).astype(F32)
    low = row - high - middle
    place = lax.broadcasted_iota(jnp.int32, (count, row.shape[1]), 0)
    return jnp.where(
        place == 0, high, jnp.where(place == 1, middle, jnp.where(place == 2, low, 0.0))
    )


def joined(three):
    three = three.astype(F32)
    return three[0:1, :] + (three[1:2, :] + three[2:3, :])


def call(kernel, operands, out_shape, name, scratch=()):
    here = pl.BlockSpec(memory_space=pltpu.VMEM)
    scalars = pl.BlockSpec(memory_space=pltpu.SMEM)
    return pl.pallas_call(
        kernel,
        out_shape=out_shape,
        in_specs=[scalars if operand.shape == (3,) else here for operand in operands],
        out_specs=(here,) * len(out_shape),
        scratch_shapes=list(scratch),
        name=name,
        compiler_params=pltpu.CompilerParams(vmem_limit_bytes=VMEM_LIMIT),
    )(*operands)


def prepare_kernel(
    capacity,
    group,
    place_ref,
    q_ref,
    it_ref,
    ng_ref,
    id_ref,
    ng_id_ref,
    ng_count_ref,
    owner_ref,
    slot_ref,
    mem_ref,
    block_ref,
    copies_ref,
    sh_ref,
    z_ref,
    y_ref,
    own_ref,
):
    rows, negs = q_ref.shape[0], ng_ref.shape[0]
    keys = rows + negs
    extra = block_ref.shape[0] - rows - keys
    sh_ref[:, 0:rows] = -jnp.log(rows * group * sample_chance(id_ref[...]))
    sh_ref[:, rows:] = jnp.log(ng_count_ref[...].astype(F32)) - jnp.log(
        negs * group * sample_chance(ng_id_ref[...])
    )
    block_ref[0:rows, :] = q_ref[...]
    block_ref[rows : 2 * rows, :] = it_ref[...]
    block_ref[2 * rows : rows + keys, :] = ng_ref[...]
    block_ref[rows + keys :, :] = jnp.zeros((extra, block_ref.shape[1]), BF16)
    block_ref[rows + keys :, 0:keys] = split_rows(sh_ref[...], extra).astype(BF16)

    pairs = copies_ref.shape[0]
    for k in range(pairs):
        copies_ref[k] = q_ref[...]
    count = it_ref.shape[0]
    own_int = owner_ref[...]
    own_row = own_int.astype(F32)
    own_col = to_column(own_row)
    earlier = lax.broadcasted_iota(jnp.int32, (count, count), 0) < lax.broadcasted_iota(
        jnp.int32, (count, count), 1
    )
    rank = jnp.sum(
        jnp.where(jnp.logical_and(own_col == own_row, earlier), 1.0, 0.0), axis=0, keepdims=True
    ).astype(jnp.int32)
    half = own_int // (2 * pairs)
    depth = own_int - half * (2 * pairs)
    pair = depth // 2
    parity = depth - pair * 2
    other = jnp.where(half == place_ref[0], 0, 2) + jnp.where(parity == place_ref[1], 0, 1)
    target = (other * pairs + pair) * capacity + rank
    places = pairs * 4 * capacity
    chosen = jnp.where(
        lax.broadcasted_iota(jnp.int32, (places, count), 0) == target, 1.0, 0.0
    ).astype(BF16)
    slot = slot_ref[...]
    high = to_column((slot >> 5).astype(F32))
    low = to_column((slot & 31).astype(F32))
    lane = lax.broadcasted_iota(jnp.int32, (count, 128), 1).astype(F32)
    lane = lane - 8.0 * to_column((other // 2).astype(F32))
    details = jnp.where(
        lane == 0.0, high, jnp.where(lane == 1.0, low, jnp.where(lane == 2.0, 1.0, 0.0))
    )
    each = places // 4
    held = mem_ref.shape[0]
    z_ref[0:held, :] = mem_ref[...]
    y_ref[0:held, :] = mem_ref[...]
    for c, (ref, at) in enumerate(
        ((own_ref, 0), (z_ref, held), (y_ref, held), (z_ref, held + each + each // 2))
    ):
        some = chosen[c * each : (c + 1) * each, :]
        ref[at : at + each, :] = dot_plain(some, it_ref[...]).astype(BF16)
        slots = dot_plain(some, details.astype(BF16)).astype(BF16)
        ref[at + each : at + each + each // 2, 0:128] = slots[0 : each // 2, :]
        ref[at + each : at + each + each // 2, 128:256] = slots[each // 2 :, :]


def update_kernel(block, each, place_ref, got_ref, mem_ref, new_ref):
    rows, width = mem_ref.shape
    pairs = got_ref.shape[0]
    two = 2 * each
    items = jnp.concatenate(
        [
            got_ref[k, block + (1 + n) * two : block + (2 + n) * two, :]
            for n in range(2)
            for k in range(pairs)
        ],
        axis=0,
    )
    details = jnp.transpose(
        jnp.concatenate(
            [got_ref[k, block : block + two, block:].astype(F32) for k in range(pairs)], axis=0
        )
    )
    high, low, valid = (
        jnp.concatenate([details[n : n + 1, :], details[8 + n : 9 + n, :]], axis=1)
        for n in range(3)
    )
    slot = jnp.where(valid > 0.5, high * 32.0 + low, -1.0).astype(jnp.int32)
    places = items.shape[0]
    entry = lax.broadcasted_iota(jnp.int32, (1, places), 1)
    flipped = entry // (pairs * two)
    inside = entry - flipped * (pairs * two)
    pair = inside // two
    inside = inside - pair * two
    crossed = inside // each
    rank = inside - crossed * each
    half = jnp.where(flipped == 1, 1 - place_ref[0], place_ref[0])
    parity = jnp.where(crossed == 1, 1 - place_ref[1], place_ref[1])
    arrival = (((half * pairs + pair) * 2 + parity) * each + rank).astype(F32)
    step = 256
    for start in range(0, rows, step):
        row = lax.broadcasted_iota(jnp.int32, (step, places), 0) + start
        latest = jnp.max(jnp.where(row == slot, arrival, -1.0), axis=1, keepdims=True)
        chosen = jnp.where(arrival == latest, 1.0, 0.0).astype(BF16)
        fresh = dot_plain(chosen, items)
        old = mem_ref[start : start + step, :].astype(F32)
        new_ref[start : start + step, :] = jnp.where(latest >= 0.0, fresh, old).astype(BF16)


def memory_kernel(tile, *refs):
    q_ref, own_ref, mem_ref, z_ref, y_ref, zy_ref, out_ref = refs
    mem_refs = (mem_ref, z_ref, y_ref, zy_ref)
    held = mem_ref.shape[0]
    pairs, block, width = q_ref.shape
    span = own_ref.shape[0]
    total = span * 2 // 3
    each = total // pairs
    extra = 2 * each
    sources = ((own_ref, 0), (z_ref, held), (y_ref, held), (zy_ref, held + span))
    for k in range(0, pairs, 2):
        items, slots = [], []
        for ref, at in sources:
            items.append(ref[at + k * each : at + (k + 2) * each, :].astype(F32))
            row, side = (k * each) % (total // 2), (k * each) // (total // 2) * 128
            slots.append(
                ref[at + total + row : at + total + row + extra, side : side + 128].astype(F32)
            )
        for n in range(2):
            cut = slice(n * each, (n + 1) * each)
            for h in range(2):
                out_ref[k + n, block + (1 + h) * extra : block + (2 + h) * extra, :] = (
                    jnp.concatenate([items[2 * h][cut], items[2 * h + 1][cut]], axis=0)
                ).astype(BF16)
            out_ref[k + n, block : block + extra, block:] = jnp.concatenate(
                [slots[0][cut] + slots[2][cut], slots[1][cut] + slots[3][cut]], axis=0
            ).astype(BF16)
    step = 1024
    pieces, open_piece = [], []
    for ref in mem_refs:
        for at in range(0, held, step):
            open_piece.append(ref[at : at + step, :])
            if sum(p.shape[0] for p in open_piece) >= step:
                pieces.append(jnp.concatenate(open_piece, axis=0))
                open_piece = []

    def one_tile(n, carry):
        q = jnp.concatenate(
            [q_ref[n * (tile // block) + h, 0:block, :] for h in range(tile // block)], axis=0
        )
        top = jnp.full((tile, 1), -jnp.inf, F32)
        total = jnp.zeros((tile, 1), F32)
        acc = jnp.zeros(q.shape, F32)
        following = dot_rows(q, pieces[0])
        for k, rows in enumerate(pieces):
            s = following
            if k + 1 < len(pieces):
                following = dot_rows(q, pieces[k + 1])
            newest = jnp.maximum(top, jnp.max(s, axis=1, keepdims=True))
            p = jnp.exp(s - newest)
            scale = jnp.exp(top - newest)
            total = total * scale + jnp.sum(p, axis=1, keepdims=True)
            acc = acc * scale + dot_plain(p.astype(BF16), rows)
            top = newest
        average = (acc / total).astype(BF16)
        lse = top + jnp.log(total)
        for h in range(tile // block):
            at = n * (tile // block) + h
            out_ref[at, 0:block, :] = average[h * block : (h + 1) * block, :]
            lse_row = to_row(lse[h * block : (h + 1) * block, :])
            out_ref[at, block : block + extra, 0:block] = split_rows(lse_row, extra).astype(BF16)
        return carry

    lax.fori_loop(0, q_ref.shape[0] * block // tile, one_tile, 0)


def batch_kernel(*refs):
    *g_refs, q_ref, it_ref, sh_ref, out_ref, stat_ref, s_ref = refs
    rows = q_ref.shape[0]
    keys = sh_ref.shape[1]
    blocks = [(ref, k) for ref in g_refs for k in range(ref.shape[0])]
    q = q_ref[...]
    highest = None
    for n, (ref, k) in enumerate(blocks):
        shift = joined(ref[k, rows + keys :, 0:keys])
        s = dot_rows(q, ref[k, rows : rows + keys, :]) + shift
        s_ref[n] = s
        highest = s if highest is None else jnp.maximum(highest, s)
    top = jnp.max(highest, axis=1, keepdims=True)
    total = jnp.zeros((rows, keys), F32)
    acc = jnp.zeros(q.shape, F32)
    for n, (ref, k) in enumerate(blocks):
        p = jnp.exp(s_ref[n] - top)
        total = total + p
        acc = acc + dot_plain(p.astype(BF16), ref[k, rows : rows + keys, :])
    total = jnp.sum(total, axis=1, keepdims=True)
    out_ref[...] = acc / total
    stat_ref[0:1, :] = to_row(top + jnp.log(total))
    own = dot_rows(q, it_ref[...]) + sh_ref[:, 0:rows]
    stat_ref[1:2, :] = jnp.sum(jnp.where(eye(rows), own, 0.0), axis=0, keepdims=True)


def total_kernel(parts_ref, stat_ref, total_ref, loss_ref):
    rows = total_ref.shape[1]
    shards = parts_ref.shape[0]
    batch = stat_ref[0:1, :]
    lse = [joined(parts_ref[k, rows : rows + 16, 0:rows]) for k in range(shards)]
    top = batch
    for row in lse:
        top = jnp.maximum(top, row)
    summed = jnp.exp(batch - top)
    for row in lse:
        summed = summed + jnp.exp(row - top)
    log_total = top + jnp.log(summed)
    total_ref[...] = log_total
    loss_ref[...] = log_total - stat_ref[1:2, :]


def item_kernel(*refs):
    place_ref, *g_refs, lt_ref, q_ref, it_ref, ng_ref, sh_ref, item_ref, neg_ref = refs
    rows = q_ref.shape[0]
    here = place_ref[2]
    near = g_refs[0].shape[0]
    peers = sum(ref.shape[0] for ref in g_refs)
    keys = jnp.concatenate([it_ref[...], ng_ref[...]], axis=0)
    shift = to_column(sh_ref[...])
    acc = jnp.zeros(keys.shape, F32)
    low = lax.rem(here, near)
    blocks = [(ref, k) for ref in g_refs for k in range(ref.shape[0])]
    for at in range(0, peers, 2):
        base = lax.rem(here - low - (at // near) * near + peers, peers)
        pair = blocks[at : at + 2]
        queries = jnp.concatenate([ref[k, 0:rows, :] for ref, k in pair], axis=0)
        log_total = jnp.concatenate(
            [lt_ref[pl.ds(base + (low ^ ((at + n) % near)), 1), :] for n in range(2)], axis=1
        )
        w = jnp.exp(dot_rows(keys, queries) + shift - log_total).astype(BF16)
        acc = acc + dot_plain(w, queries)
    item_ref[...] = acc[0:rows, :] - q_ref[...].astype(F32)
    neg_ref[...] = acc[rows:, :]


def query_kernel(parts_ref, lt_ref, batch_ref, stat_ref, it_ref, out_ref):
    log_total = lt_ref[...]
    rows = log_total.shape[1]
    out = batch_ref[...] * to_column(jnp.exp(stat_ref[0:1, :] - log_total))
    for k in range(parts_ref.shape[0]):
        share = to_column(jnp.exp(joined(parts_ref[k, rows : rows + 16, 0:rows]) - log_total))
        out = out + parts_ref[k, 0:rows, :].astype(F32) * share
    out_ref[...] = out - it_ref[...].astype(F32)


def local(
    query_vectors,
    item_vectors,
    negative_vectors,
    item_ids,
    negative_ids,
    negative_counts,
    memory,
    owners,
    memory_slots,
):
    rows, width = query_vectors.shape
    negatives = negative_vectors.shape[0]
    keys = rows + negatives
    mem = memory[0]
    group = lax.axis_size("dp")
    shards = lax.axis_size("zh")
    depth = shards * lax.axis_size("zl")
    cycle = depth * lax.axis_size("yh")
    column = ("yh", "zh", "zl")

    def beside(block, over, by):
        route = [
            (y * depth + z, ((y + over) % 2) * depth + (z ^ by))
            for y in range(cycle // depth)
            for z in range(depth)
        ]
        return lax.ppermute(block, column, route)

    place = jnp.stack([lax.axis_index("yh"), lax.axis_index("zl"), lax.axis_index("dp")])
    capacity = max(2, 2 * rows // cycle)
    held = mem.shape[0]
    span = shards * capacity * 3 // 2
    block, copies, shift, z_sent, y_sent, own_items = call(
        lambda *refs: prepare_kernel(capacity, group, *refs),
        (
            place,
            query_vectors,
            item_vectors,
            negative_vectors,
            item_ids[None, :],
            negative_ids[None, :],
            negative_counts[None, :],
            owners.reshape(1, rows),
            memory_slots[None, :],
            mem,
        ),
        (
            jax.ShapeDtypeStruct((rows + keys + 16, width), BF16),
            jax.ShapeDtypeStruct((shards, rows, width), BF16),
            jax.ShapeDtypeStruct((1, keys), F32),
            jax.ShapeDtypeStruct((held + 2 * span, width), BF16),
            jax.ShapeDtypeStruct((held + span, width), BF16),
            jax.ShapeDtypeStruct((span, width), BF16),
        ),
        "prepare",
    )
    near = 4
    near_blocks = [block] + [
        lax.ppermute(block, "dp", [(i, i ^ k) for i in range(group)]) for k in range(1, near)
    ]
    pair_blocks = jnp.stack(near_blocks)
    z_rows = beside(z_sent, 0, 1)
    y_rows = beside(y_sent, 1, 0)
    copies, z_rows, y_rows, pair_blocks = lax.optimization_barrier(
        (copies, z_rows, y_rows, pair_blocks)
    )
    zy_rows = beside(z_rows, 1, 0)
    memory_blocks = [own_items, mem, z_rows, y_rows, zy_rows]
    arrived = lax.all_to_all(copies, "zh", 0, 0, tiled=True)

    def along(blocks, by):
        return lax.ppermute(blocks, "dp", [(i, (i + near * by) % group) for i in range(group)])

    before, after = along(pair_blocks, 1), along(pair_blocks, -1)
    arrived, before, after, memory_blocks = lax.optimization_barrier(
        (arrived, before, after, memory_blocks)
    )

    (parts,) = call(
        lambda *refs: memory_kernel(512, *refs),
        (arrived, *memory_blocks),
        (jax.ShapeDtypeStruct((shards, rows + 6 * capacity, width), BF16),),
        "memory",
    )
    parts, before, after = lax.optimization_barrier((parts, before, after))
    parts_back = lax.all_to_all(parts, "zh", 0, 0, tiled=True)

    group_blocks = [
        pair_blocks,
        before,
        along(before[: near // 2], 1),
        along(after[near // 2 :], -1),
        after,
    ]
    batch_part, batch_stat = call(
        batch_kernel,
        (*group_blocks, query_vectors, item_vectors, shift),
        (
            jax.ShapeDtypeStruct((rows, width), F32),
            jax.ShapeDtypeStruct((2, rows), F32),
        ),
        "batch",
        [pltpu.VMEM((group, rows, keys), F32)],
    )
    parts_back, batch_part, batch_stat = lax.optimization_barrier(
        (parts_back, batch_part, batch_stat)
    )
    log_total, loss = call(
        total_kernel,
        (parts_back, batch_stat),
        (jax.ShapeDtypeStruct((1, rows), F32), jax.ShapeDtypeStruct((1, rows), F32)),
        "total",
    )
    group_totals = lax.all_to_all(
        jnp.broadcast_to(log_total[None], (group, 1, rows)), "dp", 0, 0, tiled=True
    ).reshape(group, rows)
    (query_grad,) = call(
        query_kernel,
        (parts_back, log_total, batch_part, batch_stat, item_vectors),
        (jax.ShapeDtypeStruct((rows, width), F32),),
        "queries",
    )
    (updated,) = call(
        lambda *refs: update_kernel(rows, capacity, *refs),
        (place, parts_back, mem),
        (jax.ShapeDtypeStruct(mem.shape, BF16),),
        "update",
    )
    group_totals, query_grad, updated = lax.optimization_barrier(
        (group_totals, query_grad, updated)
    )
    item_grad, negative_grad = call(
        item_kernel,
        (
            place,
            *group_blocks,
            group_totals,
            query_vectors,
            item_vectors,
            negative_vectors,
            shift,
        ),
        (
            jax.ShapeDtypeStruct((rows, width), F32),
            jax.ShapeDtypeStruct((negatives, width), F32),
        ),
        "items",
    )
    return (loss[0], query_grad, item_grad, negative_grad, updated[None])


def solution(mesh):
    cycle, group = mesh.shape["mem"], mesh.shape["dp"]
    cut = Mesh(
        mesh.devices.reshape(2, cycle // 4, 2, group), ("yh", "zh", "zl", "dp")
    )
    spread = ("yh", "zh", "zl", "dp")
    column = ("yh", "zh", "zl")
    return jax.shard_map(
        local,
        mesh=cut,
        in_specs=(
            P(spread, None),
            P(spread, None),
            P(spread, None),
            P(spread),
            P(spread),
            P(spread),
            P("dp", column, None),
            P(spread, None),
            P(spread),
        ),
        out_specs=(
            P(spread),
            P(spread, None),
            P(spread, None),
            P(spread, None),
            P("dp", column, None),
        ),
        check_vma=False,
    )
```

```python
import math

import jax
import jax.numpy as jnp
from jax import lax
from jax.experimental import pallas as pl
from jax.experimental.pallas import tpu as pltpu
from jax.sharding import Mesh, PartitionSpec as P

ITEMS = 65536
BF16 = jnp.bfloat16
F32 = jnp.float32
VMEM_LIMIT = 56 * 1024 * 1024


def sample_chance(identities):
    return jnp.log1p(1.0 / (identities.astype(F32) + 1.0)) / math.log(ITEMS + 1)


def dot_rows(left, right):
    return lax.dot_general(left, right, (((1,), (1,)), ((), ())), preferred_element_type=F32)


def dot_plain(left, right):
    return jnp.dot(left, right, preferred_element_type=F32)


def eye(size):
    return lax.broadcasted_iota(jnp.int32, (size, size), 0) == lax.broadcasted_iota(
        jnp.int32, (size, size), 1
    )


def to_row(column):
    return jnp.sum(jnp.where(eye(column.shape[0]), column, 0), axis=0, keepdims=True)


def to_column(row):
    return jnp.sum(jnp.where(eye(row.shape[1]), row, 0), axis=1, keepdims=True)


def split_rows(row, count):
    high = row.astype(BF16).astype(F32)
    middle = (row - high).astype(BF16).astype(F32)
    low = row - high - middle
    place = lax.broadcasted_iota(jnp.int32, (count, row.shape[1]), 0)
    return jnp.where(
        place == 0, high, jnp.where(place == 1, middle, jnp.where(place == 2, low, 0.0))
    )


def joined(three):
    three = three.astype(F32)
    return three[0:1, :] + (three[1:2, :] + three[2:3, :])


def call(kernel, operands, out_shape, name, scratch=()):
    here = pl.BlockSpec(memory_space=pltpu.VMEM)
    scalars = pl.BlockSpec(memory_space=pltpu.SMEM)
    return pl.pallas_call(
        kernel,
        out_shape=out_shape,
        in_specs=[scalars if operand.shape == (2,) else here for operand in operands],
        out_specs=(here,) * len(out_shape),
        scratch_shapes=list(scratch),
        name=name,
        compiler_params=pltpu.CompilerParams(vmem_limit_bytes=VMEM_LIMIT),
    )(*operands)


def prepare_kernel(
    capacity,
    group,
    pairs,
    place_ref,
    q_ref,
    it_ref,
    ng_ref,
    id_ref,
    ng_id_ref,
    ng_count_ref,
    owner_ref,
    slot_ref,
    mem_ref,
    block_ref,
    sh_ref,
    z_ref,
    y_ref,
    own_ref,
):
    rows, negs = q_ref.shape[0], ng_ref.shape[0]
    keys = rows + negs
    extra = block_ref.shape[1] - rows - keys
    sh_ref[:, 0:rows] = -jnp.log(rows * group * sample_chance(id_ref[...]))
    sh_ref[:, rows:] = jnp.log(ng_count_ref[...].astype(F32)) - jnp.log(
        negs * group * sample_chance(ng_id_ref[...])
    )
    shifts = split_rows(sh_ref[...], extra).astype(BF16)
    for k in range(group):
        block_ref[k, 0:rows, :] = q_ref[...]
        block_ref[k, rows : 2 * rows, :] = it_ref[...]
        block_ref[k, 2 * rows : rows + keys, :] = ng_ref[...]
        block_ref[k, rows + keys :, 0:keys] = shifts
        block_ref[k, rows + keys :, keys:] = jnp.zeros(
            (extra, block_ref.shape[2] - keys), BF16
        )

    count = it_ref.shape[0]
    own_int = owner_ref[...]
    own_row = own_int.astype(F32)
    own_col = to_column(own_row)
    earlier = lax.broadcasted_iota(jnp.int32, (count, count), 0) < lax.broadcasted_iota(
        jnp.int32, (count, count), 1
    )
    rank = jnp.sum(
        jnp.where(jnp.logical_and(own_col == own_row, earlier), 1.0, 0.0), axis=0, keepdims=True
    ).astype(jnp.int32)
    half = own_int // (2 * pairs)
    depth = own_int - half * (2 * pairs)
    pair = depth // 2
    parity = depth - pair * 2
    other = jnp.where(half == place_ref[0], 0, 2) + jnp.where(parity == place_ref[1], 0, 1)
    target = (other * pairs + pair) * capacity + rank
    places = pairs * 4 * capacity
    chosen = jnp.where(
        lax.broadcasted_iota(jnp.int32, (places, count), 0) == target, 1.0, 0.0
    ).astype(BF16)
    slot = slot_ref[...]
    high = to_column((slot >> 5).astype(F32))
    low = to_column((slot & 31).astype(F32))
    lane = lax.broadcasted_iota(jnp.int32, (count, 128), 1).astype(F32)
    lane = lane - 8.0 * to_column((other // 2).astype(F32))
    details = jnp.where(
        lane == 0.0, high, jnp.where(lane == 1.0, low, jnp.where(lane == 2.0, 1.0, 0.0))
    )
    each = places // 4
    held = mem_ref.shape[0]
    z_ref[0:held, :] = mem_ref[...]
    y_ref[0:held, :] = mem_ref[...]
    for c, (ref, at) in enumerate(
        ((own_ref, 0), (z_ref, held), (y_ref, held), (z_ref, held + each + each // 2))
    ):
        some = chosen[c * each : (c + 1) * each, :]
        ref[at : at + each, :] = dot_plain(some, it_ref[...]).astype(BF16)
        slots = dot_plain(some, details.astype(BF16)).astype(BF16)
        ref[at + each : at + each + each // 2, 0:128] = slots[0 : each // 2, :]
        ref[at + each : at + each + each // 2, 128:256] = slots[each // 2 :, :]


def update_kernel(block, each, place_ref, got_ref, mem_ref, new_ref):
    rows, width = mem_ref.shape
    pairs = got_ref.shape[0]
    two = 2 * each
    items = jnp.concatenate(
        [
            got_ref[k, block + (1 + n) * two : block + (2 + n) * two, :]
            for n in range(2)
            for k in range(pairs)
        ],
        axis=0,
    )
    details = jnp.transpose(
        jnp.concatenate(
            [got_ref[k, block : block + two, block:].astype(F32) for k in range(pairs)], axis=0
        )
    )
    high, low, valid = (
        jnp.concatenate([details[n : n + 1, :], details[8 + n : 9 + n, :]], axis=1)
        for n in range(3)
    )
    slot = jnp.where(valid > 0.5, high * 32.0 + low, -1.0).astype(jnp.int32)
    places = items.shape[0]
    entry = lax.broadcasted_iota(jnp.int32, (1, places), 1)
    flipped = entry // (pairs * two)
    inside = entry - flipped * (pairs * two)
    pair = inside // two
    inside = inside - pair * two
    crossed = inside // each
    rank = inside - crossed * each
    half = jnp.where(flipped == 1, 1 - place_ref[0], place_ref[0])
    parity = jnp.where(crossed == 1, 1 - place_ref[1], place_ref[1])
    arrival = (((half * pairs + pair) * 2 + parity) * each + rank).astype(F32)
    step = 256
    for start in range(0, rows, step):
        row = lax.broadcasted_iota(jnp.int32, (step, places), 0) + start
        latest = jnp.max(jnp.where(row == slot, arrival, -1.0), axis=1, keepdims=True)
        chosen = jnp.where(arrival == latest, 1.0, 0.0).astype(BF16)
        fresh = dot_plain(chosen, items)
        old = mem_ref[start : start + step, :].astype(F32)
        new_ref[start : start + step, :] = jnp.where(latest >= 0.0, fresh, old).astype(BF16)


def memory_kernel(tile, *refs):
    q_ref, own_ref, mem_ref, z_ref, y_ref, zy_ref, out_ref = refs
    mem_refs = (mem_ref, z_ref, y_ref, zy_ref)
    held = mem_ref.shape[0]
    pairs, block, width = q_ref.shape
    span = own_ref.shape[0]
    total = span * 2 // 3
    each = total // pairs
    extra = 2 * each
    sources = ((own_ref, 0), (z_ref, held), (y_ref, held), (zy_ref, held + span))
    for k in range(0, pairs, 2):
        items, slots = [], []
        for ref, at in sources:
            items.append(ref[at + k * each : at + (k + 2) * each, :].astype(F32))
            row, side = (k * each) % (total // 2), (k * each) // (total // 2) * 128
            slots.append(
                ref[at + total + row : at + total + row + extra, side : side + 128].astype(F32)
            )
        for n in range(2):
            cut = slice(n * each, (n + 1) * each)
            for h in range(2):
                out_ref[k + n, block + (1 + h) * extra : block + (2 + h) * extra, :] = (
                    jnp.concatenate([items[2 * h][cut], items[2 * h + 1][cut]], axis=0)
                ).astype(BF16)
            out_ref[k + n, block : block + extra, block:] = jnp.concatenate(
                [slots[0][cut] + slots[2][cut], slots[1][cut] + slots[3][cut]], axis=0
            ).astype(BF16)
    step = 1024
    pieces, open_piece = [], []
    for ref in mem_refs:
        for at in range(0, held, step):
            open_piece.append(ref[at : at + step, :])
            if sum(p.shape[0] for p in open_piece) >= step:
                pieces.append(jnp.concatenate(open_piece, axis=0))
                open_piece = []

    def one_tile(n, carry):
        q = jnp.concatenate(
            [q_ref[n * (tile // block) + h, 0:block, :] for h in range(tile // block)], axis=0
        )
        top = jnp.full((tile, 1), -jnp.inf, F32)
        total = jnp.zeros((tile, 1), F32)
        acc = jnp.zeros(q.shape, F32)
        following = dot_rows(q, pieces[0])
        for k, rows in enumerate(pieces):
            s = following
            if k + 1 < len(pieces):
                following = dot_rows(q, pieces[k + 1])
            newest = jnp.maximum(top, jnp.max(s, axis=1, keepdims=True))
            p = jnp.exp(s - newest)
            scale = jnp.exp(top - newest)
            total = total * scale + jnp.sum(p, axis=1, keepdims=True)
            acc = acc * scale + dot_plain(p.astype(BF16), rows)
            top = newest
        average = (acc / total).astype(BF16)
        lse = top + jnp.log(total)
        for h in range(tile // block):
            at = n * (tile // block) + h
            out_ref[at, 0:block, :] = average[h * block : (h + 1) * block, :]
            lse_row = to_row(lse[h * block : (h + 1) * block, :])
            out_ref[at, block : block + extra, 0:block] = split_rows(lse_row, extra).astype(BF16)
        return carry

    lax.fori_loop(0, q_ref.shape[0] * block // tile, one_tile, 0)


def batch_kernel(g_ref, q_ref, it_ref, sh_ref, out_ref, stat_ref, s_ref):
    rows = q_ref.shape[0]
    keys = sh_ref.shape[1]
    q = q_ref[...]
    highest = None
    for k in range(g_ref.shape[0]):
        shift = joined(g_ref[k, rows + keys :, 0:keys])
        s = dot_rows(q, g_ref[k, rows : rows + keys, :]) + shift
        s_ref[k] = s
        highest = s if highest is None else jnp.maximum(highest, s)
    top = jnp.max(highest, axis=1, keepdims=True)
    total = jnp.zeros((rows, keys), F32)
    acc = jnp.zeros(q.shape, F32)
    for k in range(g_ref.shape[0]):
        p = jnp.exp(s_ref[k] - top)
        total = total + p
        acc = acc + dot_plain(p.astype(BF16), g_ref[k, rows : rows + keys, :])
    total = jnp.sum(total, axis=1, keepdims=True)
    out_ref[...] = acc / total
    stat_ref[0:1, :] = to_row(top + jnp.log(total))
    own = dot_rows(q, it_ref[...]) + sh_ref[:, 0:rows]
    stat_ref[1:2, :] = jnp.sum(jnp.where(eye(rows), own, 0.0), axis=0, keepdims=True)


def total_kernel(parts_ref, stat_ref, total_ref, loss_ref):
    rows = total_ref.shape[1]
    shards = parts_ref.shape[0]
    batch = stat_ref[0:1, :]
    lse = [joined(parts_ref[k, rows : rows + 16, 0:rows]) for k in range(shards)]
    top = batch
    for row in lse:
        top = jnp.maximum(top, row)
    summed = jnp.exp(batch - top)
    for row in lse:
        summed = summed + jnp.exp(row - top)
    log_total = top + jnp.log(summed)
    total_ref[...] = log_total
    loss_ref[...] = log_total - stat_ref[1:2, :]


def item_kernel(g_ref, lt_ref, q_ref, it_ref, ng_ref, sh_ref, item_ref, neg_ref):
    rows = q_ref.shape[0]
    keys = jnp.concatenate([it_ref[...], ng_ref[...]], axis=0)
    shift = to_column(sh_ref[...])
    acc = jnp.zeros(keys.shape, F32)
    for k in range(0, g_ref.shape[0], 2):
        queries = jnp.concatenate([g_ref[k + n, 0:rows, :] for n in range(2)], axis=0)
        log_total = jnp.concatenate([lt_ref[k + n : k + n + 1, :] for n in range(2)], axis=1)
        w = jnp.exp(dot_rows(keys, queries) + shift - log_total).astype(BF16)
        acc = acc + dot_plain(w, queries)
    item_ref[...] = acc[0:rows, :] - q_ref[...].astype(F32)
    neg_ref[...] = acc[rows:, :]


def query_kernel(parts_ref, lt_ref, batch_ref, stat_ref, it_ref, out_ref):
    log_total = lt_ref[...]
    rows = log_total.shape[1]
    out = batch_ref[...] * to_column(jnp.exp(stat_ref[0:1, :] - log_total))
    for k in range(parts_ref.shape[0]):
        share = to_column(jnp.exp(joined(parts_ref[k, rows : rows + 16, 0:rows]) - log_total))
        out = out + parts_ref[k, 0:rows, :].astype(F32) * share
    out_ref[...] = out - it_ref[...].astype(F32)


def local(
    query_vectors,
    item_vectors,
    negative_vectors,
    item_ids,
    negative_ids,
    negative_counts,
    memory,
    owners,
    memory_slots,
):
    rows, width = query_vectors.shape
    negatives = negative_vectors.shape[0]
    keys = rows + negatives
    mem = memory[0]
    group = lax.axis_size("dp")
    shards = lax.axis_size("zh")
    depth = shards * lax.axis_size("zl")
    cycle = depth * lax.axis_size("yh")
    column = ("yh", "zh", "zl")

    def beside(block, over, by):
        route = [
            (y * depth + z, ((y + over) % 2) * depth + (z ^ by))
            for y in range(cycle // depth)
            for z in range(depth)
        ]
        return lax.ppermute(block, column, route)

    place = jnp.stack([lax.axis_index("yh"), lax.axis_index("zl")])
    capacity = max(2, 2 * rows // cycle)
    held = mem.shape[0]
    span = shards * capacity * 3 // 2
    block, shift, z_sent, y_sent, own_items = call(
        lambda *refs: prepare_kernel(capacity, group, shards, *refs),
        (
            place,
            query_vectors,
            item_vectors,
            negative_vectors,
            item_ids[None, :],
            negative_ids[None, :],
            negative_counts[None, :],
            owners.reshape(1, rows),
            memory_slots[None, :],
            mem,
        ),
        (
            jax.ShapeDtypeStruct((group, rows + keys + 16, width), BF16),
            jax.ShapeDtypeStruct((1, keys), F32),
            jax.ShapeDtypeStruct((held + 2 * span, width), BF16),
            jax.ShapeDtypeStruct((held + span, width), BF16),
            jax.ShapeDtypeStruct((span, width), BF16),
        ),
        "prepare",
    )
    gathered = lax.all_to_all(block, "dp", 0, 0, tiled=True)
    z_rows = beside(z_sent, 0, 1)
    y_rows = beside(y_sent, 1, 0)
    z_rows, queries = lax.optimization_barrier((z_rows, query_vectors))
    zy_rows = beside(z_rows, 1, 0)
    memory_blocks = [own_items, mem, z_rows, y_rows, zy_rows]
    arrived = lax.all_gather(queries, "zh", axis=0, tiled=False)

    (parts,) = call(
        lambda *refs: memory_kernel(512, *refs),
        (arrived, *memory_blocks),
        (jax.ShapeDtypeStruct((shards, rows + 6 * capacity, width), BF16),),
        "memory",
    )
    parts, gathered = lax.optimization_barrier((parts, gathered))
    parts_back = lax.all_to_all(parts, "zh", 0, 0, tiled=True)

    batch_part, batch_stat = call(
        batch_kernel,
        (gathered, query_vectors, item_vectors, shift),
        (
            jax.ShapeDtypeStruct((rows, width), F32),
            jax.ShapeDtypeStruct((2, rows), F32),
        ),
        "batch",
        [pltpu.VMEM((group, rows, keys), F32)],
    )
    parts_back, batch_part, batch_stat = lax.optimization_barrier(
        (parts_back, batch_part, batch_stat)
    )
    log_total, loss = call(
        total_kernel,
        (parts_back, batch_stat),
        (jax.ShapeDtypeStruct((1, rows), F32), jax.ShapeDtypeStruct((1, rows), F32)),
        "total",
    )
    group_totals = lax.all_to_all(
        jnp.broadcast_to(log_total[None], (group, 1, rows)), "dp", 0, 0, tiled=True
    ).reshape(group, rows)
    (query_grad,) = call(
        query_kernel,
        (parts_back, log_total, batch_part, batch_stat, item_vectors),
        (jax.ShapeDtypeStruct((rows, width), F32),),
        "queries",
    )
    (updated,) = call(
        lambda *refs: update_kernel(rows, capacity, *refs),
        (place, parts_back, mem),
        (jax.ShapeDtypeStruct(mem.shape, BF16),),
        "update",
    )
    group_totals, query_grad, updated = lax.optimization_barrier(
        (group_totals, query_grad, updated)
    )
    item_grad, negative_grad = call(
        item_kernel,
        (
            gathered,
            group_totals,
            query_vectors,
            item_vectors,
            negative_vectors,
            shift,
        ),
        (
            jax.ShapeDtypeStruct((rows, width), F32),
            jax.ShapeDtypeStruct((negatives, width), F32),
        ),
        "items",
    )
    return (loss[0], query_grad, item_grad, negative_grad, updated[None])


def solution(mesh):
    cycle, group = mesh.shape["mem"], mesh.shape["dp"]
    cut = Mesh(
        mesh.devices.reshape(2, cycle // 4, 2, group), ("yh", "zh", "zl", "dp")
    )
    spread = ("yh", "zh", "zl", "dp")
    column = ("yh", "zh", "zl")
    return jax.shard_map(
        local,
        mesh=cut,
        in_specs=(
            P(spread, None),
            P(spread, None),
            P(spread, None),
            P(spread),
            P(spread),
            P(spread),
            P("dp", column, None),
            P(spread, None),
            P(spread),
        ),
        out_specs=(
            P(spread),
            P(spread, None),
            P(spread, None),
            P(spread, None),
            P("dp", column, None),
        ),
        check_vma=False,
    )
```

```python
import math

import jax
import jax.numpy as jnp
from jax import lax
from jax.experimental import pallas as pl
from jax.experimental.pallas import tpu as pltpu
from jax.sharding import Mesh, PartitionSpec as P

ITEMS = 65536
BF16 = jnp.bfloat16
F32 = jnp.float32
VMEM_LIMIT = 56 * 1024 * 1024


def sample_chance(identities):
    return jnp.log1p(1.0 / (identities.astype(F32) + 1.0)) / math.log(ITEMS + 1)


def dot_rows(left, right):
    return lax.dot_general(left, right, (((1,), (1,)), ((), ())), preferred_element_type=F32)


def dot_plain(left, right):
    return jnp.dot(left, right, preferred_element_type=F32)


def eye(size):
    return lax.broadcasted_iota(jnp.int32, (size, size), 0) == lax.broadcasted_iota(
        jnp.int32, (size, size), 1
    )


def to_row(column):
    return jnp.sum(jnp.where(eye(column.shape[0]), column, 0), axis=0, keepdims=True)


def to_column(row):
    return jnp.sum(jnp.where(eye(row.shape[1]), row, 0), axis=1, keepdims=True)


def split_rows(row, count):
    high = row.astype(BF16).astype(F32)
    middle = (row - high).astype(BF16).astype(F32)
    low = row - high - middle
    place = lax.broadcasted_iota(jnp.int32, (count, row.shape[1]), 0)
    return jnp.where(
        place == 0, high, jnp.where(place == 1, middle, jnp.where(place == 2, low, 0.0))
    )


def joined(three):
    three = three.astype(F32)
    return three[0:1, :] + (three[1:2, :] + three[2:3, :])


def call(kernel, operands, out_shape, name, scratch=()):
    here = pl.BlockSpec(memory_space=pltpu.VMEM)
    scalars = pl.BlockSpec(memory_space=pltpu.SMEM)
    return pl.pallas_call(
        kernel,
        out_shape=out_shape,
        in_specs=[scalars if operand.shape == (2,) else here for operand in operands],
        out_specs=(here,) * len(out_shape),
        scratch_shapes=list(scratch),
        name=name,
        compiler_params=pltpu.CompilerParams(vmem_limit_bytes=VMEM_LIMIT),
    )(*operands)


def prepare_kernel(
    capacity,
    group,
    pairs,
    place_ref,
    q_ref,
    it_ref,
    ng_ref,
    id_ref,
    ng_id_ref,
    ng_count_ref,
    owner_ref,
    slot_ref,
    mem_ref,
    block_ref,
    sh_ref,
    z_ref,
    y_ref,
    zy_ref,
    own_ref,
):
    rows, negs = q_ref.shape[0], ng_ref.shape[0]
    keys = rows + negs
    extra = block_ref.shape[1] - rows - keys
    sh_ref[:, 0:rows] = -jnp.log(rows * group * sample_chance(id_ref[...]))
    sh_ref[:, rows:] = jnp.log(ng_count_ref[...].astype(F32)) - jnp.log(
        negs * group * sample_chance(ng_id_ref[...])
    )
    shifts = split_rows(sh_ref[...], extra).astype(BF16)
    for k in range(group):
        block_ref[k, 0:rows, :] = q_ref[...]
        block_ref[k, rows : 2 * rows, :] = it_ref[...]
        block_ref[k, 2 * rows : rows + keys, :] = ng_ref[...]
        block_ref[k, rows + keys :, 0:keys] = shifts
        block_ref[k, rows + keys :, keys:] = jnp.zeros(
            (extra, block_ref.shape[2] - keys), BF16
        )

    count = it_ref.shape[0]
    own_int = owner_ref[...]
    own_row = own_int.astype(F32)
    own_col = to_column(own_row)
    earlier = lax.broadcasted_iota(jnp.int32, (count, count), 0) < lax.broadcasted_iota(
        jnp.int32, (count, count), 1
    )
    rank = jnp.sum(
        jnp.where(jnp.logical_and(own_col == own_row, earlier), 1.0, 0.0), axis=0, keepdims=True
    ).astype(jnp.int32)
    half = own_int // (2 * pairs)
    depth = own_int - half * (2 * pairs)
    pair = depth // 2
    parity = depth - pair * 2
    other = jnp.where(half == place_ref[0], 0, 2) + jnp.where(parity == place_ref[1], 0, 1)
    target = (other * pairs + pair) * capacity + rank
    places = pairs * 4 * capacity
    chosen = jnp.where(
        lax.broadcasted_iota(jnp.int32, (places, count), 0) == target, 1.0, 0.0
    ).astype(BF16)
    slot = slot_ref[...]
    high = to_column((slot >> 5).astype(F32))
    low = to_column((slot & 31).astype(F32))
    lane = lax.broadcasted_iota(jnp.int32, (count, 128), 1).astype(F32)
    lane = lane - 8.0 * to_column((other // 2).astype(F32))
    details = jnp.where(
        lane == 0.0, high, jnp.where(lane == 1.0, low, jnp.where(lane == 2.0, 1.0, 0.0))
    )
    each = places // 4
    held = mem_ref.shape[0]
    for ref in (z_ref, y_ref, zy_ref):
        ref[0:held, :] = mem_ref[...]
    for c, (ref, at) in enumerate(((own_ref, 0), (z_ref, held), (y_ref, held), (zy_ref, held))):
        some = chosen[c * each : (c + 1) * each, :]
        ref[at : at + each, :] = dot_plain(some, it_ref[...]).astype(BF16)
        slots = dot_plain(some, details.astype(BF16)).astype(BF16)
        ref[at + each : at + each + each // 2, 0:128] = slots[0 : each // 2, :]
        ref[at + each : at + each + each // 2, 128:256] = slots[each // 2 :, :]


def update_kernel(block, each, place_ref, got_ref, mem_ref, new_ref):
    rows, width = mem_ref.shape
    pairs = got_ref.shape[0]
    two = 2 * each
    items = jnp.concatenate(
        [
            got_ref[k, block + (1 + n) * two : block + (2 + n) * two, :]
            for n in range(2)
            for k in range(pairs)
        ],
        axis=0,
    )
    details = jnp.transpose(
        jnp.concatenate(
            [got_ref[k, block : block + two, block:].astype(F32) for k in range(pairs)], axis=0
        )
    )
    high, low, valid = (
        jnp.concatenate([details[n : n + 1, :], details[8 + n : 9 + n, :]], axis=1)
        for n in range(3)
    )
    slot = jnp.where(valid > 0.5, high * 32.0 + low, -1.0).astype(jnp.int32)
    places = items.shape[0]
    entry = lax.broadcasted_iota(jnp.int32, (1, places), 1)
    flipped = entry // (pairs * two)
    inside = entry - flipped * (pairs * two)
    pair = inside // two
    inside = inside - pair * two
    crossed = inside // each
    rank = inside - crossed * each
    half = jnp.where(flipped == 1, 1 - place_ref[0], place_ref[0])
    parity = jnp.where(crossed == 1, 1 - place_ref[1], place_ref[1])
    arrival = (((half * pairs + pair) * 2 + parity) * each + rank).astype(F32)
    step = 256
    for start in range(0, rows, step):
        row = lax.broadcasted_iota(jnp.int32, (step, places), 0) + start
        latest = jnp.max(jnp.where(row == slot, arrival, -1.0), axis=1, keepdims=True)
        chosen = jnp.where(arrival == latest, 1.0, 0.0).astype(BF16)
        fresh = dot_plain(chosen, items)
        old = mem_ref[start : start + step, :].astype(F32)
        new_ref[start : start + step, :] = jnp.where(latest >= 0.0, fresh, old).astype(BF16)


def memory_kernel(tile, *refs):
    q_ref, own_ref, mem_ref, z_ref, y_ref, zy_ref, out_ref = refs
    mem_refs = (mem_ref, z_ref, y_ref, zy_ref)
    held = mem_ref.shape[0]
    pairs, block, width = q_ref.shape
    span = own_ref.shape[0]
    total = span * 2 // 3
    each = total // pairs
    extra = 2 * each
    sources = ((own_ref, 0), (z_ref, held), (y_ref, held), (zy_ref, held))
    for k in range(0, pairs, 2):
        items, slots = [], []
        for ref, at in sources:
            items.append(ref[at + k * each : at + (k + 2) * each, :].astype(F32))
            row, side = (k * each) % (total // 2), (k * each) // (total // 2) * 128
            slots.append(
                ref[at + total + row : at + total + row + extra, side : side + 128].astype(F32)
            )
        for n in range(2):
            cut = slice(n * each, (n + 1) * each)
            for h in range(2):
                out_ref[k + n, block + (1 + h) * extra : block + (2 + h) * extra, :] = (
                    jnp.concatenate([items[2 * h][cut], items[2 * h + 1][cut]], axis=0)
                ).astype(BF16)
            out_ref[k + n, block : block + extra, block:] = jnp.concatenate(
                [slots[0][cut] + slots[2][cut], slots[1][cut] + slots[3][cut]], axis=0
            ).astype(BF16)
    step = 1024
    pieces, open_piece = [], []
    for ref in mem_refs:
        for at in range(0, held, step):
            open_piece.append(ref[at : at + step, :])
            if sum(p.shape[0] for p in open_piece) >= step:
                pieces.append(jnp.concatenate(open_piece, axis=0))
                open_piece = []

    def one_tile(n, carry):
        q = jnp.concatenate(
            [q_ref[n * (tile // block) + h, 0:block, :] for h in range(tile // block)], axis=0
        )
        top = jnp.full((tile, 1), -jnp.inf, F32)
        total = jnp.zeros((tile, 1), F32)
        acc = jnp.zeros(q.shape, F32)
        following = dot_rows(q, pieces[0])
        for k, rows in enumerate(pieces):
            s = following
            if k + 1 < len(pieces):
                following = dot_rows(q, pieces[k + 1])
            newest = jnp.maximum(top, jnp.max(s, axis=1, keepdims=True))
            p = jnp.exp(s - newest)
            scale = jnp.exp(top - newest)
            total = total * scale + jnp.sum(p, axis=1, keepdims=True)
            acc = acc * scale + dot_plain(p.astype(BF16), rows)
            top = newest
        average = (acc / total).astype(BF16)
        lse = top + jnp.log(total)
        for h in range(tile // block):
            at = n * (tile // block) + h
            out_ref[at, 0:block, :] = average[h * block : (h + 1) * block, :]
            lse_row = to_row(lse[h * block : (h + 1) * block, :])
            out_ref[at, block : block + extra, 0:block] = split_rows(lse_row, extra).astype(BF16)
        return carry

    lax.fori_loop(0, q_ref.shape[0] * block // tile, one_tile, 0)


def batch_kernel(g_ref, q_ref, it_ref, sh_ref, out_ref, stat_ref, s_ref):
    rows = q_ref.shape[0]
    keys = sh_ref.shape[1]
    q = q_ref[...]
    highest = None
    for k in range(g_ref.shape[0]):
        shift = joined(g_ref[k, rows + keys :, 0:keys])
        s = dot_rows(q, g_ref[k, rows : rows + keys, :]) + shift
        s_ref[k] = s
        highest = s if highest is None else jnp.maximum(highest, s)
    top = jnp.max(highest, axis=1, keepdims=True)
    total = jnp.zeros((rows, keys), F32)
    acc = jnp.zeros(q.shape, F32)
    for k in range(g_ref.shape[0]):
        p = jnp.exp(s_ref[k] - top)
        total = total + p
        acc = acc + dot_plain(p.astype(BF16), g_ref[k, rows : rows + keys, :])
    total = jnp.sum(total, axis=1, keepdims=True)
    out_ref[...] = acc / total
    stat_ref[0:1, :] = to_row(top + jnp.log(total))
    own = dot_rows(q, it_ref[...]) + sh_ref[:, 0:rows]
    stat_ref[1:2, :] = jnp.sum(jnp.where(eye(rows), own, 0.0), axis=0, keepdims=True)


def total_kernel(parts_ref, stat_ref, total_ref, copies_ref, loss_ref):
    rows = total_ref.shape[1]
    shards = parts_ref.shape[0]
    batch = stat_ref[0:1, :]
    lse = [joined(parts_ref[k, rows : rows + 16, 0:rows]) for k in range(shards)]
    top = batch
    for row in lse:
        top = jnp.maximum(top, row)
    summed = jnp.exp(batch - top)
    for row in lse:
        summed = summed + jnp.exp(row - top)
    log_total = top + jnp.log(summed)
    total_ref[...] = log_total
    for k in range(copies_ref.shape[0]):
        copies_ref[k] = log_total
    loss_ref[...] = log_total - stat_ref[1:2, :]


def item_kernel(g_ref, lt_ref, q_ref, it_ref, ng_ref, sh_ref, item_ref, neg_ref):
    rows = q_ref.shape[0]
    keys = jnp.concatenate([it_ref[...], ng_ref[...]], axis=0)
    shift = to_column(sh_ref[...])
    acc = jnp.zeros(keys.shape, F32)
    for k in range(0, g_ref.shape[0], 2):
        queries = jnp.concatenate([g_ref[k + n, 0:rows, :] for n in range(2)], axis=0)
        log_total = jnp.concatenate([lt_ref[k + n : k + n + 1, :] for n in range(2)], axis=1)
        w = jnp.exp(dot_rows(keys, queries) + shift - log_total).astype(BF16)
        acc = acc + dot_plain(w, queries)
    item_ref[...] = acc[0:rows, :] - q_ref[...].astype(F32)
    neg_ref[...] = acc[rows:, :]


def query_kernel(parts_ref, lt_ref, batch_ref, stat_ref, it_ref, out_ref):
    log_total = lt_ref[...]
    rows = log_total.shape[1]
    out = batch_ref[...] * to_column(jnp.exp(stat_ref[0:1, :] - log_total))
    for k in range(parts_ref.shape[0]):
        share = to_column(jnp.exp(joined(parts_ref[k, rows : rows + 16, 0:rows]) - log_total))
        out = out + parts_ref[k, 0:rows, :].astype(F32) * share
    out_ref[...] = out - it_ref[...].astype(F32)


def local(
    query_vectors,
    item_vectors,
    negative_vectors,
    item_ids,
    negative_ids,
    negative_counts,
    memory,
    owners,
    memory_slots,
):
    rows, width = query_vectors.shape
    negatives = negative_vectors.shape[0]
    keys = rows + negatives
    mem = memory[0]
    group = lax.axis_size("dp")
    shards = lax.axis_size("zh")
    depth = shards * lax.axis_size("zl")
    cycle = depth * lax.axis_size("yh")
    column = ("yh", "zh", "zl")

    def beside(block, over, by):
        route = [
            (y * depth + z, ((y + over) % 2) * depth + (z ^ by))
            for y in range(cycle // depth)
            for z in range(depth)
        ]
        return lax.ppermute(block, column, route)

    place = jnp.stack([lax.axis_index("yh"), lax.axis_index("zl")])
    capacity = max(2, 2 * rows // cycle)
    held = mem.shape[0]
    span = shards * capacity * 3 // 2
    block, shift, z_sent, y_sent, zy_sent, own_items = call(
        lambda *refs: prepare_kernel(capacity, group, shards, *refs),
        (
            place,
            query_vectors,
            item_vectors,
            negative_vectors,
            item_ids[None, :],
            negative_ids[None, :],
            negative_counts[None, :],
            owners.reshape(1, rows),
            memory_slots[None, :],
            mem,
        ),
        (
            jax.ShapeDtypeStruct((group, rows + keys + 16, width), BF16),
            jax.ShapeDtypeStruct((1, keys), F32),
        )
        + (jax.ShapeDtypeStruct((held + span, width), BF16),) * 3
        + (jax.ShapeDtypeStruct((span, width), BF16),),
        "prepare",
    )
    gathered = lax.all_to_all(block, "dp", 0, 0, tiled=True)
    memory_blocks = [
        own_items,
        mem,
        beside(z_sent, 0, 1),
        beside(y_sent, 1, 0),
        beside(zy_sent, 1, 1),
    ]
    arrived = lax.all_gather(query_vectors, "zh", axis=0, tiled=False)

    (parts,) = call(
        lambda *refs: memory_kernel(512, *refs),
        (arrived, *memory_blocks),
        (jax.ShapeDtypeStruct((shards, rows + 6 * capacity, width), BF16),),
        "memory",
    )
    parts, gathered = lax.optimization_barrier((parts, gathered))
    parts_back = lax.all_to_all(parts, "zh", 0, 0, tiled=True)

    batch_part, batch_stat = call(
        batch_kernel,
        (gathered, query_vectors, item_vectors, shift),
        (
            jax.ShapeDtypeStruct((rows, width), F32),
            jax.ShapeDtypeStruct((2, rows), F32),
        ),
        "batch",
        [pltpu.VMEM((group, rows, keys), F32)],
    )
    parts_back, batch_part, batch_stat = lax.optimization_barrier(
        (parts_back, batch_part, batch_stat)
    )
    log_total, total_copies, loss = call(
        total_kernel,
        (parts_back, batch_stat),
        (
            jax.ShapeDtypeStruct((1, rows), F32),
            jax.ShapeDtypeStruct((group, 1, rows), F32),
            jax.ShapeDtypeStruct((1, rows), F32),
        ),
        "total",
    )
    group_totals = lax.all_to_all(total_copies, "dp", 0, 0, tiled=True).reshape(group, rows)
    (query_grad,) = call(
        query_kernel,
        (parts_back, log_total, batch_part, batch_stat, item_vectors),
        (jax.ShapeDtypeStruct((rows, width), F32),),
        "queries",
    )
    (updated,) = call(
        lambda *refs: update_kernel(rows, capacity, *refs),
        (place, parts_back, mem),
        (jax.ShapeDtypeStruct(mem.shape, BF16),),
        "update",
    )
    group_totals, query_grad, updated = lax.optimization_barrier(
        (group_totals, query_grad, updated)
    )
    item_grad, negative_grad = call(
        item_kernel,
        (
            gathered,
            group_totals,
            query_vectors,
            item_vectors,
            negative_vectors,
            shift,
        ),
        (
            jax.ShapeDtypeStruct((rows, width), F32),
            jax.ShapeDtypeStruct((negatives, width), F32),
        ),
        "items",
    )
    return (loss[0], query_grad, item_grad, negative_grad, updated[None])


def solution(mesh):
    cycle, group = mesh.shape["mem"], mesh.shape["dp"]
    cut = Mesh(
        mesh.devices.reshape(2, cycle // 4, 2, group), ("yh", "zh", "zl", "dp")
    )
    spread = ("yh", "zh", "zl", "dp")
    column = ("yh", "zh", "zl")
    return jax.shard_map(
        local,
        mesh=cut,
        in_specs=(
            P(spread, None),
            P(spread, None),
            P(spread, None),
            P(spread),
            P(spread),
            P(spread),
            P("dp", column, None),
            P(spread, None),
            P(spread),
        ),
        out_specs=(
            P(spread),
            P(spread, None),
            P(spread, None),
            P(spread, None),
            P("dp", column, None),
        ),
        check_vma=False,
    )
```

```python
import math

import jax
import jax.numpy as jnp
from jax import lax
from jax.experimental import pallas as pl
from jax.experimental.pallas import tpu as pltpu
from jax.sharding import Mesh, PartitionSpec as P

ITEMS = 65536
BF16 = jnp.bfloat16
F32 = jnp.float32
VMEM_LIMIT = 56 * 1024 * 1024


def sample_chance(identities):
    return jnp.log1p(1.0 / (identities.astype(F32) + 1.0)) / math.log(ITEMS + 1)


def dot_rows(left, right):
    return lax.dot_general(left, right, (((1,), (1,)), ((), ())), preferred_element_type=F32)


def dot_plain(left, right):
    return jnp.dot(left, right, preferred_element_type=F32)


def eye(size):
    return lax.broadcasted_iota(jnp.int32, (size, size), 0) == lax.broadcasted_iota(
        jnp.int32, (size, size), 1
    )


def to_row(column):
    return jnp.sum(jnp.where(eye(column.shape[0]), column, 0), axis=0, keepdims=True)


def to_column(row):
    return jnp.sum(jnp.where(eye(row.shape[1]), row, 0), axis=1, keepdims=True)


def split_rows(row, count):
    high = row.astype(BF16).astype(F32)
    middle = (row - high).astype(BF16).astype(F32)
    low = row - high - middle
    place = lax.broadcasted_iota(jnp.int32, (count, row.shape[1]), 0)
    return jnp.where(
        place == 0, high, jnp.where(place == 1, middle, jnp.where(place == 2, low, 0.0))
    )


def joined(three):
    three = three.astype(F32)
    return three[0:1, :] + (three[1:2, :] + three[2:3, :])


def call(kernel, operands, out_shape, name, scratch=()):
    here = pl.BlockSpec(memory_space=pltpu.VMEM)
    scalars = pl.BlockSpec(memory_space=pltpu.SMEM)
    return pl.pallas_call(
        kernel,
        out_shape=out_shape,
        in_specs=[scalars if operand.shape == (2,) else here for operand in operands],
        out_specs=(here,) * len(out_shape),
        scratch_shapes=list(scratch),
        name=name,
        compiler_params=pltpu.CompilerParams(vmem_limit_bytes=VMEM_LIMIT),
    )(*operands)


def prepare_kernel(
    capacity,
    group,
    pairs,
    place_ref,
    q_ref,
    it_ref,
    ng_ref,
    id_ref,
    ng_id_ref,
    ng_count_ref,
    owner_ref,
    slot_ref,
    mem_ref,
    block_ref,
    sh_ref,
    z_ref,
    y_ref,
    own_ref,
):
    rows, negs = q_ref.shape[0], ng_ref.shape[0]
    keys = rows + negs
    extra = block_ref.shape[1] - rows - keys
    sh_ref[:, 0:rows] = -jnp.log(rows * group * sample_chance(id_ref[...]))
    sh_ref[:, rows:] = jnp.log(ng_count_ref[...].astype(F32)) - jnp.log(
        negs * group * sample_chance(ng_id_ref[...])
    )
    shifts = split_rows(sh_ref[...], extra).astype(BF16)
    for k in range(group):
        block_ref[k, 0:rows, :] = q_ref[...]
        block_ref[k, rows : 2 * rows, :] = it_ref[...]
        block_ref[k, 2 * rows : rows + keys, :] = ng_ref[...]
        block_ref[k, rows + keys :, 0:keys] = shifts
        block_ref[k, rows + keys :, keys:] = jnp.zeros(
            (extra, block_ref.shape[2] - keys), BF16
        )

    count = it_ref.shape[0]
    own_int = owner_ref[...]
    own_row = own_int.astype(F32)
    own_col = to_column(own_row)
    earlier = lax.broadcasted_iota(jnp.int32, (count, count), 0) < lax.broadcasted_iota(
        jnp.int32, (count, count), 1
    )
    rank = jnp.sum(
        jnp.where(jnp.logical_and(own_col == own_row, earlier), 1.0, 0.0), axis=0, keepdims=True
    ).astype(jnp.int32)
    half = own_int // (2 * pairs)
    depth = own_int - half * (2 * pairs)
    pair = depth // 2
    parity = depth - pair * 2
    other = jnp.where(half == place_ref[0], 0, 2) + jnp.where(parity == place_ref[1], 0, 1)
    target = (other * pairs + pair) * capacity + rank
    places = pairs * 4 * capacity
    chosen = jnp.where(
        lax.broadcasted_iota(jnp.int32, (places, count), 0) == target, 1.0, 0.0
    ).astype(BF16)
    slot = slot_ref[...]
    high = to_column((slot >> 5).astype(F32))
    low = to_column((slot & 31).astype(F32))
    lane = lax.broadcasted_iota(jnp.int32, (count, 128), 1).astype(F32)
    lane = lane - 8.0 * to_column((other // 2).astype(F32))
    details = jnp.where(
        lane == 0.0, high, jnp.where(lane == 1.0, low, jnp.where(lane == 2.0, 1.0, 0.0))
    )
    each = places // 4
    held = mem_ref.shape[0]
    z_ref[0:held, :] = mem_ref[...]
    y_ref[0:held, :] = mem_ref[...]
    for c, (ref, at) in enumerate(
        ((own_ref, 0), (z_ref, held), (y_ref, held), (z_ref, held + each + each // 2))
    ):
        some = chosen[c * each : (c + 1) * each, :]
        ref[at : at + each, :] = dot_plain(some, it_ref[...]).astype(BF16)
        slots = dot_plain(some, details.astype(BF16)).astype(BF16)
        ref[at + each : at + each + each // 2, 0:128] = slots[0 : each // 2, :]
        ref[at + each : at + each + each // 2, 128:256] = slots[each // 2 :, :]


def update_kernel(block, each, place_ref, got_ref, mem_ref, new_ref):
    rows, width = mem_ref.shape
    pairs = got_ref.shape[0]
    two = 2 * each
    items = jnp.concatenate(
        [
            got_ref[k, block + (1 + n) * two : block + (2 + n) * two, :]
            for n in range(2)
            for k in range(pairs)
        ],
        axis=0,
    )
    details = jnp.transpose(
        jnp.concatenate(
            [got_ref[k, block : block + two, block:].astype(F32) for k in range(pairs)], axis=0
        )
    )
    high, low, valid = (
        jnp.concatenate([details[n : n + 1, :], details[8 + n : 9 + n, :]], axis=1)
        for n in range(3)
    )
    slot = jnp.where(valid > 0.5, high * 32.0 + low, -1.0).astype(jnp.int32)
    places = items.shape[0]
    entry = lax.broadcasted_iota(jnp.int32, (1, places), 1)
    flipped = entry // (pairs * two)
    inside = entry - flipped * (pairs * two)
    pair = inside // two
    inside = inside - pair * two
    crossed = inside // each
    rank = inside - crossed * each
    half = jnp.where(flipped == 1, 1 - place_ref[0], place_ref[0])
    parity = jnp.where(crossed == 1, 1 - place_ref[1], place_ref[1])
    arrival = (((half * pairs + pair) * 2 + parity) * each + rank).astype(F32)
    step = 256
    for start in range(0, rows, step):
        row = lax.broadcasted_iota(jnp.int32, (step, places), 0) + start
        latest = jnp.max(jnp.where(row == slot, arrival, -1.0), axis=1, keepdims=True)
        chosen = jnp.where(arrival == latest, 1.0, 0.0).astype(BF16)
        fresh = dot_plain(chosen, items)
        old = mem_ref[start : start + step, :].astype(F32)
        new_ref[start : start + step, :] = jnp.where(latest >= 0.0, fresh, old).astype(BF16)


def memory_kernel(tile, *refs):
    q_ref, own_ref, mem_ref, z_ref, y_ref, zy_ref, out_ref = refs
    mem_refs = (mem_ref, z_ref, y_ref, zy_ref)
    held = mem_ref.shape[0]
    pairs, block, width = q_ref.shape
    span = own_ref.shape[0]
    total = span * 2 // 3
    each = total // pairs
    extra = 2 * each
    sources = ((own_ref, 0), (z_ref, held), (y_ref, held), (zy_ref, held + span))
    for k in range(0, pairs, 2):
        items, slots = [], []
        for ref, at in sources:
            items.append(ref[at + k * each : at + (k + 2) * each, :].astype(F32))
            row, side = (k * each) % (total // 2), (k * each) // (total // 2) * 128
            slots.append(
                ref[at + total + row : at + total + row + extra, side : side + 128].astype(F32)
            )
        for n in range(2):
            cut = slice(n * each, (n + 1) * each)
            for h in range(2):
                out_ref[k + n, block + (1 + h) * extra : block + (2 + h) * extra, :] = (
                    jnp.concatenate([items[2 * h][cut], items[2 * h + 1][cut]], axis=0)
                ).astype(BF16)
            out_ref[k + n, block : block + extra, block:] = jnp.concatenate(
                [slots[0][cut] + slots[2][cut], slots[1][cut] + slots[3][cut]], axis=0
            ).astype(BF16)
    step = 1024
    pieces, open_piece = [], []
    for ref in mem_refs:
        for at in range(0, held, step):
            open_piece.append(ref[at : at + step, :])
            if sum(p.shape[0] for p in open_piece) >= step:
                pieces.append(jnp.concatenate(open_piece, axis=0))
                open_piece = []

    def one_tile(n, carry):
        q = jnp.concatenate(
            [q_ref[n * (tile // block) + h, 0:block, :] for h in range(tile // block)], axis=0
        )
        top = jnp.full((tile, 1), -jnp.inf, F32)
        total = jnp.zeros((tile, 1), F32)
        acc = jnp.zeros(q.shape, F32)
        following = dot_rows(q, pieces[0])
        for k, rows in enumerate(pieces):
            s = following
            if k + 1 < len(pieces):
                following = dot_rows(q, pieces[k + 1])
            newest = jnp.maximum(top, jnp.max(s, axis=1, keepdims=True))
            p = jnp.exp(s - newest)
            scale = jnp.exp(top - newest)
            total = total * scale + jnp.sum(p, axis=1, keepdims=True)
            acc = acc * scale + dot_plain(p.astype(BF16), rows)
            top = newest
        average = (acc / total).astype(BF16)
        lse = top + jnp.log(total)
        for h in range(tile // block):
            at = n * (tile // block) + h
            out_ref[at, 0:block, :] = average[h * block : (h + 1) * block, :]
            lse_row = to_row(lse[h * block : (h + 1) * block, :])
            out_ref[at, block : block + extra, 0:block] = split_rows(lse_row, extra).astype(BF16)
        return carry

    lax.fori_loop(0, q_ref.shape[0] * block // tile, one_tile, 0)


def batch_kernel(g_ref, q_ref, it_ref, sh_ref, out_ref, stat_ref, s_ref):
    rows = q_ref.shape[0]
    keys = sh_ref.shape[1]
    q = q_ref[...]
    highest = None
    for k in range(g_ref.shape[0]):
        shift = joined(g_ref[k, rows + keys :, 0:keys])
        s = dot_rows(q, g_ref[k, rows : rows + keys, :]) + shift
        s_ref[k] = s
        highest = s if highest is None else jnp.maximum(highest, s)
    top = jnp.max(highest, axis=1, keepdims=True)
    total = jnp.zeros((rows, keys), F32)
    acc = jnp.zeros(q.shape, F32)
    for k in range(g_ref.shape[0]):
        p = jnp.exp(s_ref[k] - top)
        total = total + p
        acc = acc + dot_plain(p.astype(BF16), g_ref[k, rows : rows + keys, :])
    total = jnp.sum(total, axis=1, keepdims=True)
    out_ref[...] = acc / total
    stat_ref[0:1, :] = to_row(top + jnp.log(total))
    own = dot_rows(q, it_ref[...]) + sh_ref[:, 0:rows]
    stat_ref[1:2, :] = jnp.sum(jnp.where(eye(rows), own, 0.0), axis=0, keepdims=True)


def total_kernel(parts_ref, stat_ref, total_ref, copies_ref, loss_ref):
    rows = total_ref.shape[1]
    shards = parts_ref.shape[0]
    batch = stat_ref[0:1, :]
    lse = [joined(parts_ref[k, rows : rows + 16, 0:rows]) for k in range(shards)]
    top = batch
    for row in lse:
        top = jnp.maximum(top, row)
    summed = jnp.exp(batch - top)
    for row in lse:
        summed = summed + jnp.exp(row - top)
    log_total = top + jnp.log(summed)
    total_ref[...] = log_total
    for k in range(copies_ref.shape[0]):
        copies_ref[k] = log_total
    loss_ref[...] = log_total - stat_ref[1:2, :]


def item_kernel(g_ref, lt_ref, q_ref, it_ref, ng_ref, sh_ref, item_ref, neg_ref):
    rows = q_ref.shape[0]
    keys = jnp.concatenate([it_ref[...], ng_ref[...]], axis=0)
    shift = to_column(sh_ref[...])
    acc = jnp.zeros(keys.shape, F32)
    for k in range(0, g_ref.shape[0], 2):
        queries = jnp.concatenate([g_ref[k + n, 0:rows, :] for n in range(2)], axis=0)
        log_total = jnp.concatenate([lt_ref[k + n : k + n + 1, :] for n in range(2)], axis=1)
        w = jnp.exp(dot_rows(keys, queries) + shift - log_total).astype(BF16)
        acc = acc + dot_plain(w, queries)
    item_ref[...] = acc[0:rows, :] - q_ref[...].astype(F32)
    neg_ref[...] = acc[rows:, :]


def query_kernel(parts_ref, lt_ref, batch_ref, stat_ref, it_ref, out_ref):
    log_total = lt_ref[...]
    rows = log_total.shape[1]
    out = batch_ref[...] * to_column(jnp.exp(stat_ref[0:1, :] - log_total))
    for k in range(parts_ref.shape[0]):
        share = to_column(jnp.exp(joined(parts_ref[k, rows : rows + 16, 0:rows]) - log_total))
        out = out + parts_ref[k, 0:rows, :].astype(F32) * share
    out_ref[...] = out - it_ref[...].astype(F32)


def local(
    query_vectors,
    item_vectors,
    negative_vectors,
    item_ids,
    negative_ids,
    negative_counts,
    memory,
    owners,
    memory_slots,
):
    rows, width = query_vectors.shape
    negatives = negative_vectors.shape[0]
    keys = rows + negatives
    mem = memory[0]
    group = lax.axis_size("dp")
    shards = lax.axis_size("zh")
    depth = shards * lax.axis_size("zl")
    cycle = depth * lax.axis_size("yh")
    column = ("yh", "zh", "zl")

    def beside(block, over, by):
        route = [
            (y * depth + z, ((y + over) % 2) * depth + (z ^ by))
            for y in range(cycle // depth)
            for z in range(depth)
        ]
        return lax.ppermute(block, column, route)

    place = jnp.stack([lax.axis_index("yh"), lax.axis_index("zl")])
    capacity = max(2, 2 * rows // cycle)
    held = mem.shape[0]
    span = shards * capacity * 3 // 2
    block, shift, z_sent, y_sent, own_items = call(
        lambda *refs: prepare_kernel(capacity, group, shards, *refs),
        (
            place,
            query_vectors,
            item_vectors,
            negative_vectors,
            item_ids[None, :],
            negative_ids[None, :],
            negative_counts[None, :],
            owners.reshape(1, rows),
            memory_slots[None, :],
            mem,
        ),
        (
            jax.ShapeDtypeStruct((group, rows + keys + 16, width), BF16),
            jax.ShapeDtypeStruct((1, keys), F32),
            jax.ShapeDtypeStruct((held + 2 * span, width), BF16),
            jax.ShapeDtypeStruct((held + span, width), BF16),
            jax.ShapeDtypeStruct((span, width), BF16),
        ),
        "prepare",
    )
    z_rows = beside(z_sent, 0, 1)
    y_rows = beside(y_sent, 1, 0)
    z_rows, y_rows, queries, block = lax.optimization_barrier(
        (z_rows, y_rows, query_vectors, block)
    )
    gathered = lax.all_to_all(block, "dp", 0, 0, tiled=True)
    zy_rows = beside(z_rows, 1, 0)
    memory_blocks = [own_items, mem, z_rows, y_rows, zy_rows]
    arrived = lax.all_gather(queries, "zh", axis=0, tiled=False)

    (parts,) = call(
        lambda *refs: memory_kernel(512, *refs),
        (arrived, *memory_blocks),
        (jax.ShapeDtypeStruct((shards, rows + 6 * capacity, width), BF16),),
        "memory",
    )
    parts, gathered = lax.optimization_barrier((parts, gathered))
    parts_back = lax.all_to_all(parts, "zh", 0, 0, tiled=True)

    batch_part, batch_stat = call(
        batch_kernel,
        (gathered, query_vectors, item_vectors, shift),
        (
            jax.ShapeDtypeStruct((rows, width), F32),
            jax.ShapeDtypeStruct((2, rows), F32),
        ),
        "batch",
        [pltpu.VMEM((group, rows, keys), F32)],
    )
    parts_back, batch_part, batch_stat = lax.optimization_barrier(
        (parts_back, batch_part, batch_stat)
    )
    log_total, total_copies, loss = call(
        total_kernel,
        (parts_back, batch_stat),
        (
            jax.ShapeDtypeStruct((1, rows), F32),
            jax.ShapeDtypeStruct((group, 1, rows), F32),
            jax.ShapeDtypeStruct((1, rows), F32),
        ),
        "total",
    )
    group_totals = lax.all_to_all(total_copies, "dp", 0, 0, tiled=True).reshape(group, rows)
    (query_grad,) = call(
        query_kernel,
        (parts_back, log_total, batch_part, batch_stat, item_vectors),
        (jax.ShapeDtypeStruct((rows, width), F32),),
        "queries",
    )
    (updated,) = call(
        lambda *refs: update_kernel(rows, capacity, *refs),
        (place, parts_back, mem),
        (jax.ShapeDtypeStruct(mem.shape, BF16),),
        "update",
    )
    group_totals, query_grad, updated = lax.optimization_barrier(
        (group_totals, query_grad, updated)
    )
    item_grad, negative_grad = call(
        item_kernel,
        (
            gathered,
            group_totals,
            query_vectors,
            item_vectors,
            negative_vectors,
            shift,
        ),
        (
            jax.ShapeDtypeStruct((rows, width), F32),
            jax.ShapeDtypeStruct((negatives, width), F32),
        ),
        "items",
    )
    return (loss[0], query_grad, item_grad, negative_grad, updated[None])


def solution(mesh):
    cycle, group = mesh.shape["mem"], mesh.shape["dp"]
    cut = Mesh(
        mesh.devices.reshape(2, cycle // 4, 2, group), ("yh", "zh", "zl", "dp")
    )
    spread = ("yh", "zh", "zl", "dp")
    column = ("yh", "zh", "zl")
    return jax.shard_map(
        local,
        mesh=cut,
        in_specs=(
            P(spread, None),
            P(spread, None),
            P(spread, None),
            P(spread),
            P(spread),
            P(spread),
            P("dp", column, None),
            P(spread, None),
            P(spread),
        ),
        out_specs=(
            P(spread),
            P(spread, None),
            P(spread, None),
            P(spread, None),
            P("dp", column, None),
        ),
        check_vma=False,
    )
```

```python
import math

import jax
import jax.numpy as jnp
from jax import lax
from jax.experimental import pallas as pl
from jax.experimental.pallas import tpu as pltpu
from jax.sharding import Mesh, PartitionSpec as P

ITEMS = 65536
BF16 = jnp.bfloat16
F32 = jnp.float32
VMEM_LIMIT = 56 * 1024 * 1024


def sample_chance(identities):
    return jnp.log1p(1.0 / (identities.astype(F32) + 1.0)) / math.log(ITEMS + 1)


def dot_rows(left, right):
    return lax.dot_general(left, right, (((1,), (1,)), ((), ())), preferred_element_type=F32)


def dot_plain(left, right):
    return jnp.dot(left, right, preferred_element_type=F32)


def eye(size):
    return lax.broadcasted_iota(jnp.int32, (size, size), 0) == lax.broadcasted_iota(
        jnp.int32, (size, size), 1
    )


def to_row(column):
    return jnp.sum(jnp.where(eye(column.shape[0]), column, 0), axis=0, keepdims=True)


def to_column(row):
    return jnp.sum(jnp.where(eye(row.shape[1]), row, 0), axis=1, keepdims=True)


def split_rows(row, count):
    high = row.astype(BF16).astype(F32)
    middle = (row - high).astype(BF16).astype(F32)
    low = row - high - middle
    place = lax.broadcasted_iota(jnp.int32, (count, row.shape[1]), 0)
    return jnp.where(
        place == 0, high, jnp.where(place == 1, middle, jnp.where(place == 2, low, 0.0))
    )


def joined(three):
    three = three.astype(F32)
    return three[0:1, :] + (three[1:2, :] + three[2:3, :])


def call(kernel, operands, out_shape, name, scratch=()):
    here = pl.BlockSpec(memory_space=pltpu.VMEM)
    scalars = pl.BlockSpec(memory_space=pltpu.SMEM)
    return pl.pallas_call(
        kernel,
        out_shape=out_shape,
        in_specs=[scalars if operand.shape == (3,) else here for operand in operands],
        out_specs=(here,) * len(out_shape),
        scratch_shapes=list(scratch),
        name=name,
        compiler_params=pltpu.CompilerParams(vmem_limit_bytes=VMEM_LIMIT),
    )(*operands)


def prepare_kernel(
    capacity,
    group,
    place_ref,
    q_ref,
    it_ref,
    ng_ref,
    id_ref,
    ng_id_ref,
    ng_count_ref,
    owner_ref,
    slot_ref,
    mem_ref,
    block_ref,
    copies_ref,
    sh_ref,
    z_ref,
    y_ref,
    own_ref,
):
    rows, negs = q_ref.shape[0], ng_ref.shape[0]
    keys = rows + negs
    extra = block_ref.shape[0] - rows - keys
    sh_ref[:, 0:rows] = -jnp.log(rows * group * sample_chance(id_ref[...]))
    sh_ref[:, rows:] = jnp.log(ng_count_ref[...].astype(F32)) - jnp.log(
        negs * group * sample_chance(ng_id_ref[...])
    )
    block_ref[0:rows, :] = q_ref[...]
    block_ref[rows : 2 * rows, :] = it_ref[...]
    block_ref[2 * rows : rows + keys, :] = ng_ref[...]
    block_ref[rows + keys :, :] = jnp.zeros((extra, block_ref.shape[1]), BF16)
    block_ref[rows + keys :, 0:keys] = split_rows(sh_ref[...], extra).astype(BF16)

    pairs = copies_ref.shape[0]
    for k in range(pairs):
        copies_ref[k] = q_ref[...]
    count = it_ref.shape[0]
    own_int = owner_ref[...]
    own_row = own_int.astype(F32)
    own_col = to_column(own_row)
    earlier = lax.broadcasted_iota(jnp.int32, (count, count), 0) < lax.broadcasted_iota(
        jnp.int32, (count, count), 1
    )
    rank = jnp.sum(
        jnp.where(jnp.logical_and(own_col == own_row, earlier), 1.0, 0.0), axis=0, keepdims=True
    ).astype(jnp.int32)
    half = own_int // (2 * pairs)
    depth = own_int - half * (2 * pairs)
    pair = depth // 2
    parity = depth - pair * 2
    other = jnp.where(half == place_ref[0], 0, 2) + jnp.where(parity == place_ref[1], 0, 1)
    target = (other * pairs + pair) * capacity + rank
    places = pairs * 4 * capacity
    chosen = jnp.where(
        lax.broadcasted_iota(jnp.int32, (places, count), 0) == target, 1.0, 0.0
    ).astype(BF16)
    slot = slot_ref[...]
    high = to_column((slot >> 5).astype(F32))
    low = to_column((slot & 31).astype(F32))
    lane = lax.broadcasted_iota(jnp.int32, (count, 128), 1).astype(F32)
    lane = lane - 8.0 * to_column((other // 2).astype(F32))
    details = jnp.where(
        lane == 0.0, high, jnp.where(lane == 1.0, low, jnp.where(lane == 2.0, 1.0, 0.0))
    )
    each = places // 4
    held = mem_ref.shape[0]
    z_ref[0:held, :] = mem_ref[...]
    y_ref[0:held, :] = mem_ref[...]
    for c, (ref, at) in enumerate(
        ((own_ref, 0), (z_ref, held), (y_ref, held), (z_ref, held + each + each // 2))
    ):
        some = chosen[c * each : (c + 1) * each, :]
        ref[at : at + each, :] = dot_plain(some, it_ref[...]).astype(BF16)
        slots = dot_plain(some, details.astype(BF16)).astype(BF16)
        ref[at + each : at + each + each // 2, 0:128] = slots[0 : each // 2, :]
        ref[at + each : at + each + each // 2, 128:256] = slots[each // 2 :, :]


def update_kernel(block, each, place_ref, got_ref, mem_ref, new_ref):
    rows, width = mem_ref.shape
    pairs = got_ref.shape[0]
    two = 2 * each
    items = jnp.concatenate(
        [
            got_ref[k, block + (1 + n) * two : block + (2 + n) * two, :]
            for n in range(2)
            for k in range(pairs)
        ],
        axis=0,
    )
    details = jnp.transpose(
        jnp.concatenate(
            [got_ref[k, block : block + two, block:].astype(F32) for k in range(pairs)], axis=0
        )
    )
    high, low, valid = (
        jnp.concatenate([details[n : n + 1, :], details[8 + n : 9 + n, :]], axis=1)
        for n in range(3)
    )
    slot = jnp.where(valid > 0.5, high * 32.0 + low, -1.0).astype(jnp.int32)
    places = items.shape[0]
    entry = lax.broadcasted_iota(jnp.int32, (1, places), 1)
    flipped = entry // (pairs * two)
    inside = entry - flipped * (pairs * two)
    pair = inside // two
    inside = inside - pair * two
    crossed = inside // each
    rank = inside - crossed * each
    half = jnp.where(flipped == 1, 1 - place_ref[0], place_ref[0])
    parity = jnp.where(crossed == 1, 1 - place_ref[1], place_ref[1])
    arrival = (((half * pairs + pair) * 2 + parity) * each + rank).astype(F32)
    step = 256
    for start in range(0, rows, step):
        row = lax.broadcasted_iota(jnp.int32, (step, places), 0) + start
        latest = jnp.max(jnp.where(row == slot, arrival, -1.0), axis=1, keepdims=True)
        chosen = jnp.where(arrival == latest, 1.0, 0.0).astype(BF16)
        fresh = dot_plain(chosen, items)
        old = mem_ref[start : start + step, :].astype(F32)
        new_ref[start : start + step, :] = jnp.where(latest >= 0.0, fresh, old).astype(BF16)


def memory_kernel(tile, *refs):
    q_ref, own_ref, mem_ref, z_ref, y_ref, zy_ref, out_ref = refs
    mem_refs = (mem_ref, z_ref, y_ref, zy_ref)
    held = mem_ref.shape[0]
    pairs, block, width = q_ref.shape
    span = own_ref.shape[0]
    total = span * 2 // 3
    each = total // pairs
    extra = 2 * each
    sources = ((own_ref, 0), (z_ref, held), (y_ref, held), (zy_ref, held + span))
    for k in range(0, pairs, 2):
        items, slots = [], []
        for ref, at in sources:
            items.append(ref[at + k * each : at + (k + 2) * each, :].astype(F32))
            row, side = (k * each) % (total // 2), (k * each) // (total // 2) * 128
            slots.append(
                ref[at + total + row : at + total + row + extra, side : side + 128].astype(F32)
            )
        for n in range(2):
            cut = slice(n * each, (n + 1) * each)
            for h in range(2):
                out_ref[k + n, block + (1 + h) * extra : block + (2 + h) * extra, :] = (
                    jnp.concatenate([items[2 * h][cut], items[2 * h + 1][cut]], axis=0)
                ).astype(BF16)
            out_ref[k + n, block : block + extra, block:] = jnp.concatenate(
                [slots[0][cut] + slots[2][cut], slots[1][cut] + slots[3][cut]], axis=0
            ).astype(BF16)
    step = 1024
    pieces, open_piece = [], []
    for ref in mem_refs:
        for at in range(0, held, step):
            open_piece.append(ref[at : at + step, :])
            if sum(p.shape[0] for p in open_piece) >= step:
                pieces.append(jnp.concatenate(open_piece, axis=0))
                open_piece = []

    def one_tile(n, carry):
        q = jnp.concatenate(
            [q_ref[n * (tile // block) + h, 0:block, :] for h in range(tile // block)], axis=0
        )
        top = jnp.full((tile, 1), -jnp.inf, F32)
        total = jnp.zeros((tile, 1), F32)
        acc = jnp.zeros(q.shape, F32)
        following = dot_rows(q, pieces[0])
        for k, rows in enumerate(pieces):
            s = following
            if k + 1 < len(pieces):
                following = dot_rows(q, pieces[k + 1])
            newest = jnp.maximum(top, jnp.max(s, axis=1, keepdims=True))
            p = jnp.exp(s - newest)
            scale = jnp.exp(top - newest)
            total = total * scale + jnp.sum(p, axis=1, keepdims=True)
            acc = acc * scale + dot_plain(p.astype(BF16), rows)
            top = newest
        average = (acc / total).astype(BF16)
        lse = top + jnp.log(total)
        for h in range(tile // block):
            at = n * (tile // block) + h
            out_ref[at, 0:block, :] = average[h * block : (h + 1) * block, :]
            lse_row = to_row(lse[h * block : (h + 1) * block, :])
            out_ref[at, block : block + extra, 0:block] = split_rows(lse_row, extra).astype(BF16)
        return carry

    lax.fori_loop(0, q_ref.shape[0] * block // tile, one_tile, 0)


def batch_kernel(*refs):
    *g_refs, q_ref, it_ref, sh_ref, out_ref, stat_ref, s_ref = refs
    rows = q_ref.shape[0]
    keys = sh_ref.shape[1]
    blocks = [(ref, k) for ref in g_refs for k in range(ref.shape[0])]
    q = q_ref[...]
    highest = None
    for n, (ref, k) in enumerate(blocks):
        shift = joined(ref[k, rows + keys :, 0:keys])
        s = dot_rows(q, ref[k, rows : rows + keys, :]) + shift
        s_ref[n] = s
        highest = s if highest is None else jnp.maximum(highest, s)
    top = jnp.max(highest, axis=1, keepdims=True)
    total = jnp.zeros((rows, keys), F32)
    acc = jnp.zeros(q.shape, F32)
    for n, (ref, k) in enumerate(blocks):
        p = jnp.exp(s_ref[n] - top)
        total = total + p
        acc = acc + dot_plain(p.astype(BF16), ref[k, rows : rows + keys, :])
    total = jnp.sum(total, axis=1, keepdims=True)
    out_ref[...] = acc / total
    stat_ref[0:1, :] = to_row(top + jnp.log(total))
    own = dot_rows(q, it_ref[...]) + sh_ref[:, 0:rows]
    stat_ref[1:2, :] = jnp.sum(jnp.where(eye(rows), own, 0.0), axis=0, keepdims=True)


def total_kernel(parts_ref, stat_ref, total_ref, copies_ref, loss_ref):
    rows = total_ref.shape[1]
    shards = parts_ref.shape[0]
    batch = stat_ref[0:1, :]
    lse = [joined(parts_ref[k, rows : rows + 16, 0:rows]) for k in range(shards)]
    top = batch
    for row in lse:
        top = jnp.maximum(top, row)
    summed = jnp.exp(batch - top)
    for row in lse:
        summed = summed + jnp.exp(row - top)
    log_total = top + jnp.log(summed)
    total_ref[...] = log_total
    for k in range(copies_ref.shape[0]):
        copies_ref[k] = log_total
    loss_ref[...] = log_total - stat_ref[1:2, :]


def item_kernel(*refs):
    place_ref, *g_refs, lt_ref, q_ref, it_ref, ng_ref, sh_ref, item_ref, neg_ref = refs
    rows = q_ref.shape[0]
    here = place_ref[2]
    near = g_refs[0].shape[0]
    peers = sum(ref.shape[0] for ref in g_refs)
    keys = jnp.concatenate([it_ref[...], ng_ref[...]], axis=0)
    shift = to_column(sh_ref[...])
    acc = jnp.zeros(keys.shape, F32)
    low = lax.rem(here, near)
    blocks = [(ref, k) for ref in g_refs for k in range(ref.shape[0])]
    for at in range(0, peers, 2):
        base = lax.rem(here - low - (at // near) * near + peers, peers)
        pair = blocks[at : at + 2]
        queries = jnp.concatenate([ref[k, 0:rows, :] for ref, k in pair], axis=0)
        log_total = jnp.concatenate(
            [lt_ref[pl.ds(base + (low ^ ((at + n) % near)), 1), :] for n in range(2)], axis=1
        )
        w = jnp.exp(dot_rows(keys, queries) + shift - log_total).astype(BF16)
        acc = acc + dot_plain(w, queries)
    item_ref[...] = acc[0:rows, :] - q_ref[...].astype(F32)
    neg_ref[...] = acc[rows:, :]


def query_kernel(parts_ref, lt_ref, batch_ref, stat_ref, it_ref, out_ref):
    log_total = lt_ref[...]
    rows = log_total.shape[1]
    out = batch_ref[...] * to_column(jnp.exp(stat_ref[0:1, :] - log_total))
    for k in range(parts_ref.shape[0]):
        share = to_column(jnp.exp(joined(parts_ref[k, rows : rows + 16, 0:rows]) - log_total))
        out = out + parts_ref[k, 0:rows, :].astype(F32) * share
    out_ref[...] = out - it_ref[...].astype(F32)


def local(
    query_vectors,
    item_vectors,
    negative_vectors,
    item_ids,
    negative_ids,
    negative_counts,
    memory,
    owners,
    memory_slots,
):
    rows, width = query_vectors.shape
    negatives = negative_vectors.shape[0]
    keys = rows + negatives
    mem = memory[0]
    group = lax.axis_size("dp")
    shards = lax.axis_size("zh")
    depth = shards * lax.axis_size("zl")
    cycle = depth * lax.axis_size("yh")
    column = ("yh", "zh", "zl")

    def beside(block, over, by):
        route = [
            (y * depth + z, ((y + over) % 2) * depth + (z ^ by))
            for y in range(cycle // depth)
            for z in range(depth)
        ]
        return lax.ppermute(block, column, route)

    place = jnp.stack([lax.axis_index("yh"), lax.axis_index("zl"), lax.axis_index("dp")])
    capacity = max(2, 2 * rows // cycle)
    held = mem.shape[0]
    span = shards * capacity * 3 // 2
    block, copies, shift, z_sent, y_sent, own_items = call(
        lambda *refs: prepare_kernel(capacity, group, *refs),
        (
            place,
            query_vectors,
            item_vectors,
            negative_vectors,
            item_ids[None, :],
            negative_ids[None, :],
            negative_counts[None, :],
            owners.reshape(1, rows),
            memory_slots[None, :],
            mem,
        ),
        (
            jax.ShapeDtypeStruct((rows + keys + 16, width), BF16),
            jax.ShapeDtypeStruct((shards, rows, width), BF16),
            jax.ShapeDtypeStruct((1, keys), F32),
            jax.ShapeDtypeStruct((held + 2 * span, width), BF16),
            jax.ShapeDtypeStruct((held + span, width), BF16),
            jax.ShapeDtypeStruct((span, width), BF16),
        ),
        "prepare",
    )
    near = 4
    near_blocks = [block] + [
        lax.ppermute(block, "dp", [(i, i ^ k) for i in range(group)]) for k in range(1, near)
    ]
    pair_blocks = jnp.stack(near_blocks)
    z_rows = beside(z_sent, 0, 1)
    y_rows = beside(y_sent, 1, 0)
    copies, z_rows, pair_blocks = lax.optimization_barrier((copies, z_rows, pair_blocks))
    zy_rows = beside(z_rows, 1, 0)
    memory_blocks = [own_items, mem, z_rows, y_rows, zy_rows]
    arrived = lax.all_to_all(copies, "zh", 0, 0, tiled=True)

    def along(blocks, by):
        return lax.ppermute(blocks, "dp", [(i, (i + near * by) % group) for i in range(group)])

    before, after = along(pair_blocks, 1), along(pair_blocks, -1)
    arrived, before, after, memory_blocks = lax.optimization_barrier(
        (arrived, before, after, memory_blocks)
    )

    (parts,) = call(
        lambda *refs: memory_kernel(512, *refs),
        (arrived, *memory_blocks),
        (jax.ShapeDtypeStruct((shards, rows + 6 * capacity, width), BF16),),
        "memory",
    )
    parts, before, after = lax.optimization_barrier((parts, before, after))
    parts_back = lax.all_to_all(parts, "zh", 0, 0, tiled=True)

    group_blocks = [
        pair_blocks,
        before,
        along(before[: near // 2], 1),
        along(after[near // 2 :], -1),
        after,
    ]
    batch_part, batch_stat = call(
        batch_kernel,
        (*group_blocks, query_vectors, item_vectors, shift),
        (
            jax.ShapeDtypeStruct((rows, width), F32),
            jax.ShapeDtypeStruct((2, rows), F32),
        ),
        "batch",
        [pltpu.VMEM((group, rows, keys), F32)],
    )
    parts_back, batch_part, batch_stat = lax.optimization_barrier(
        (parts_back, batch_part, batch_stat)
    )
    log_total, total_copies, loss = call(
        total_kernel,
        (parts_back, batch_stat),
        (
            jax.ShapeDtypeStruct((1, rows), F32),
            jax.ShapeDtypeStruct((group, 1, rows), F32),
            jax.ShapeDtypeStruct((1, rows), F32),
        ),
        "total",
    )
    group_totals = lax.all_to_all(total_copies, "dp", 0, 0, tiled=True).reshape(group, rows)
    (query_grad,) = call(
        query_kernel,
        (parts_back, log_total, batch_part, batch_stat, item_vectors),
        (jax.ShapeDtypeStruct((rows, width), F32),),
        "queries",
    )
    (updated,) = call(
        lambda *refs: update_kernel(rows, capacity, *refs),
        (place, parts_back, mem),
        (jax.ShapeDtypeStruct(mem.shape, BF16),),
        "update",
    )
    group_totals, query_grad, updated = lax.optimization_barrier(
        (group_totals, query_grad, updated)
    )
    item_grad, negative_grad = call(
        item_kernel,
        (
            place,
            *group_blocks,
            group_totals,
            query_vectors,
            item_vectors,
            negative_vectors,
            shift,
        ),
        (
            jax.ShapeDtypeStruct((rows, width), F32),
            jax.ShapeDtypeStruct((negatives, width), F32),
        ),
        "items",
    )
    return (loss[0], query_grad, item_grad, negative_grad, updated[None])


def solution(mesh):
    cycle, group = mesh.shape["mem"], mesh.shape["dp"]
    cut = Mesh(
        mesh.devices.reshape(2, cycle // 4, 2, group), ("yh", "zh", "zl", "dp")
    )
    spread = ("yh", "zh", "zl", "dp")
    column = ("yh", "zh", "zl")
    return jax.shard_map(
        local,
        mesh=cut,
        in_specs=(
            P(spread, None),
            P(spread, None),
            P(spread, None),
            P(spread),
            P(spread),
            P(spread),
            P("dp", column, None),
            P(spread, None),
            P(spread),
        ),
        out_specs=(
            P(spread),
            P(spread, None),
            P(spread, None),
            P(spread, None),
            P("dp", column, None),
        ),
        check_vma=False,
    )
```

```python
import math

import jax
import jax.numpy as jnp
from jax import lax
from jax.experimental import pallas as pl
from jax.experimental.pallas import tpu as pltpu
from jax.sharding import Mesh, PartitionSpec as P

ITEMS = 65536
BF16 = jnp.bfloat16
F32 = jnp.float32
VMEM_LIMIT = 56 * 1024 * 1024


def sample_chance(identities):
    return jnp.log1p(1.0 / (identities.astype(F32) + 1.0)) / math.log(ITEMS + 1)


def dot_rows(left, right):
    return lax.dot_general(left, right, (((1,), (1,)), ((), ())), preferred_element_type=F32)


def dot_plain(left, right):
    return jnp.dot(left, right, preferred_element_type=F32)


def eye(size):
    return lax.broadcasted_iota(jnp.int32, (size, size), 0) == lax.broadcasted_iota(
        jnp.int32, (size, size), 1
    )


def to_row(column):
    return jnp.sum(jnp.where(eye(column.shape[0]), column, 0), axis=0, keepdims=True)


def to_column(row):
    return jnp.sum(jnp.where(eye(row.shape[1]), row, 0), axis=1, keepdims=True)


def split_rows(row, count):
    high = row.astype(BF16).astype(F32)
    middle = (row - high).astype(BF16).astype(F32)
    low = row - high - middle
    place = lax.broadcasted_iota(jnp.int32, (count, row.shape[1]), 0)
    return jnp.where(
        place == 0, high, jnp.where(place == 1, middle, jnp.where(place == 2, low, 0.0))
    )


def joined(three):
    three = three.astype(F32)
    return three[0:1, :] + (three[1:2, :] + three[2:3, :])


def call(kernel, operands, out_shape, name, scratch=()):
    here = pl.BlockSpec(memory_space=pltpu.VMEM)
    scalars = pl.BlockSpec(memory_space=pltpu.SMEM)
    return pl.pallas_call(
        kernel,
        out_shape=out_shape,
        in_specs=[scalars if operand.shape == (3,) else here for operand in operands],
        out_specs=(here,) * len(out_shape),
        scratch_shapes=list(scratch),
        name=name,
        compiler_params=pltpu.CompilerParams(vmem_limit_bytes=VMEM_LIMIT),
    )(*operands)


def prepare_kernel(
    capacity,
    group,
    place_ref,
    q_ref,
    it_ref,
    ng_ref,
    id_ref,
    ng_id_ref,
    ng_count_ref,
    owner_ref,
    slot_ref,
    mem_ref,
    block_ref,
    copies_ref,
    sh_ref,
    z_ref,
    y_ref,
    own_ref,
):
    rows, negs = q_ref.shape[0], ng_ref.shape[0]
    keys = rows + negs
    extra = block_ref.shape[0] - rows - keys
    sh_ref[:, 0:rows] = -jnp.log(rows * group * sample_chance(id_ref[...]))
    sh_ref[:, rows:] = jnp.log(ng_count_ref[...].astype(F32)) - jnp.log(
        negs * group * sample_chance(ng_id_ref[...])
    )
    block_ref[0:rows, :] = q_ref[...]
    block_ref[rows : 2 * rows, :] = it_ref[...]
    block_ref[2 * rows : rows + keys, :] = ng_ref[...]
    block_ref[rows + keys :, :] = jnp.zeros((extra, block_ref.shape[1]), BF16)
    block_ref[rows + keys :, 0:keys] = split_rows(sh_ref[...], extra).astype(BF16)

    pairs = copies_ref.shape[0]
    for k in range(pairs):
        copies_ref[k] = q_ref[...]
    count = it_ref.shape[0]
    own_int = owner_ref[...]
    own_row = own_int.astype(F32)
    own_col = to_column(own_row)
    earlier = lax.broadcasted_iota(jnp.int32, (count, count), 0) < lax.broadcasted_iota(
        jnp.int32, (count, count), 1
    )
    rank = jnp.sum(
        jnp.where(jnp.logical_and(own_col == own_row, earlier), 1.0, 0.0), axis=0, keepdims=True
    ).astype(jnp.int32)
    half = own_int // (2 * pairs)
    depth = own_int - half * (2 * pairs)
    pair = depth // 2
    parity = depth - pair * 2
    other = jnp.where(half == place_ref[0], 0, 2) + jnp.where(parity == place_ref[1], 0, 1)
    target = (other * pairs + pair) * capacity + rank
    places = pairs * 4 * capacity
    chosen = jnp.where(
        lax.broadcasted_iota(jnp.int32, (places, count), 0) == target, 1.0, 0.0
    ).astype(BF16)
    slot = slot_ref[...]
    high = to_column((slot >> 5).astype(F32))
    low = to_column((slot & 31).astype(F32))
    lane = lax.broadcasted_iota(jnp.int32, (count, 128), 1).astype(F32)
    lane = lane - 8.0 * to_column((other // 2).astype(F32))
    details = jnp.where(
        lane == 0.0, high, jnp.where(lane == 1.0, low, jnp.where(lane == 2.0, 1.0, 0.0))
    )
    each = places // 4
    held = mem_ref.shape[0]
    z_ref[0:held, :] = mem_ref[...]
    y_ref[0:held, :] = mem_ref[...]
    for c, (ref, at) in enumerate(
        ((own_ref, 0), (z_ref, held + each + each // 2), (y_ref, held), (z_ref, held))
    ):
        some = chosen[c * each : (c + 1) * each, :]
        ref[at : at + each, :] = dot_plain(some, it_ref[...]).astype(BF16)
        slots = dot_plain(some, details.astype(BF16)).astype(BF16)
        ref[at + each : at + each + each // 2, 0:128] = slots[0 : each // 2, :]
        ref[at + each : at + each + each // 2, 128:256] = slots[each // 2 :, :]


def update_kernel(block, each, place_ref, got_ref, mem_ref, new_ref):
    rows, width = mem_ref.shape
    pairs = got_ref.shape[0]
    two = 2 * each
    items = jnp.concatenate(
        [
            got_ref[k, block + (1 + n) * two : block + (2 + n) * two, :]
            for n in range(2)
            for k in range(pairs)
        ],
        axis=0,
    )
    details = jnp.transpose(
        jnp.concatenate(
            [got_ref[k, block : block + two, block:].astype(F32) for k in range(pairs)], axis=0
        )
    )
    high, low, valid = (
        jnp.concatenate([details[n : n + 1, :], details[8 + n : 9 + n, :]], axis=1)
        for n in range(3)
    )
    slot = jnp.where(valid > 0.5, high * 32.0 + low, -1.0).astype(jnp.int32)
    places = items.shape[0]
    entry = lax.broadcasted_iota(jnp.int32, (1, places), 1)
    flipped = entry // (pairs * two)
    inside = entry - flipped * (pairs * two)
    pair = inside // two
    inside = inside - pair * two
    crossed = inside // each
    rank = inside - crossed * each
    half = jnp.where(flipped == 1, 1 - place_ref[0], place_ref[0])
    parity = jnp.where(crossed == 1, 1 - place_ref[1], place_ref[1])
    arrival = (((half * pairs + pair) * 2 + parity) * each + rank).astype(F32)
    step = 256
    for start in range(0, rows, step):
        row = lax.broadcasted_iota(jnp.int32, (step, places), 0) + start
        latest = jnp.max(jnp.where(row == slot, arrival, -1.0), axis=1, keepdims=True)
        chosen = jnp.where(arrival == latest, 1.0, 0.0).astype(BF16)
        fresh = dot_plain(chosen, items)
        old = mem_ref[start : start + step, :].astype(F32)
        new_ref[start : start + step, :] = jnp.where(latest >= 0.0, fresh, old).astype(BF16)


def memory_kernel(tile, *refs):
    q_ref, own_ref, mem_ref, z_ref, y_ref, zy_ref, out_ref = refs
    mem_refs = (mem_ref, z_ref, y_ref, zy_ref)
    held = mem_ref.shape[0]
    pairs, block, width = q_ref.shape
    span = own_ref.shape[0]
    total = span * 2 // 3
    each = total // pairs
    extra = 2 * each
    sources = ((own_ref, 0), (z_ref, held + span), (y_ref, held), (zy_ref, held))
    for k in range(0, pairs, 2):
        items, slots = [], []
        for ref, at in sources:
            items.append(ref[at + k * each : at + (k + 2) * each, :].astype(F32))
            row, side = (k * each) % (total // 2), (k * each) // (total // 2) * 128
            slots.append(
                ref[at + total + row : at + total + row + extra, side : side + 128].astype(F32)
            )
        for n in range(2):
            cut = slice(n * each, (n + 1) * each)
            for h in range(2):
                out_ref[k + n, block + (1 + h) * extra : block + (2 + h) * extra, :] = (
                    jnp.concatenate([items[2 * h][cut], items[2 * h + 1][cut]], axis=0)
                ).astype(BF16)
            out_ref[k + n, block : block + extra, block:] = jnp.concatenate(
                [slots[0][cut] + slots[2][cut], slots[1][cut] + slots[3][cut]], axis=0
            ).astype(BF16)
    step = 1024
    pieces, open_piece = [], []
    for ref in mem_refs:
        for at in range(0, held, step):
            open_piece.append(ref[at : at + step, :])
            if sum(p.shape[0] for p in open_piece) >= step:
                pieces.append(jnp.concatenate(open_piece, axis=0))
                open_piece = []

    def one_tile(n, carry):
        q = jnp.concatenate(
            [q_ref[n * (tile // block) + h, 0:block, :] for h in range(tile // block)], axis=0
        )
        top = jnp.full((tile, 1), -jnp.inf, F32)
        total = jnp.zeros((tile, 1), F32)
        acc = jnp.zeros(q.shape, F32)
        following = dot_rows(q, pieces[0])
        for k, rows in enumerate(pieces):
            s = following
            if k + 1 < len(pieces):
                following = dot_rows(q, pieces[k + 1])
            newest = jnp.maximum(top, jnp.max(s, axis=1, keepdims=True))
            p = jnp.exp(s - newest)
            scale = jnp.exp(top - newest)
            total = total * scale + jnp.sum(p, axis=1, keepdims=True)
            acc = acc * scale + dot_plain(p.astype(BF16), rows)
            top = newest
        average = (acc / total).astype(BF16)
        lse = top + jnp.log(total)
        for h in range(tile // block):
            at = n * (tile // block) + h
            out_ref[at, 0:block, :] = average[h * block : (h + 1) * block, :]
            lse_row = to_row(lse[h * block : (h + 1) * block, :])
            out_ref[at, block : block + extra, 0:block] = split_rows(lse_row, extra).astype(BF16)
        return carry

    lax.fori_loop(0, q_ref.shape[0] * block // tile, one_tile, 0)


def batch_kernel(*refs):
    *g_refs, q_ref, it_ref, sh_ref, out_ref, stat_ref, s_ref = refs
    rows = q_ref.shape[0]
    keys = sh_ref.shape[1]
    blocks = [(ref, k) for ref in g_refs for k in range(ref.shape[0])]
    q = q_ref[...]
    highest = None
    for n, (ref, k) in enumerate(blocks):
        shift = joined(ref[k, rows + keys :, 0:keys])
        s = dot_rows(q, ref[k, rows : rows + keys, :]) + shift
        s_ref[n] = s
        highest = s if highest is None else jnp.maximum(highest, s)
    top = jnp.max(highest, axis=1, keepdims=True)
    total = jnp.zeros((rows, keys), F32)
    acc = jnp.zeros(q.shape, F32)
    for n, (ref, k) in enumerate(blocks):
        p = jnp.exp(s_ref[n] - top)
        total = total + p
        acc = acc + dot_plain(p.astype(BF16), ref[k, rows : rows + keys, :])
    total = jnp.sum(total, axis=1, keepdims=True)
    out_ref[...] = acc / total
    stat_ref[0:1, :] = to_row(top + jnp.log(total))
    own = dot_rows(q, it_ref[...]) + sh_ref[:, 0:rows]
    stat_ref[1:2, :] = jnp.sum(jnp.where(eye(rows), own, 0.0), axis=0, keepdims=True)


def total_kernel(parts_ref, stat_ref, total_ref, copies_ref, loss_ref):
    rows = total_ref.shape[1]
    shards = parts_ref.shape[0]
    batch = stat_ref[0:1, :]
    lse = [joined(parts_ref[k, rows : rows + 16, 0:rows]) for k in range(shards)]
    top = batch
    for row in lse:
        top = jnp.maximum(top, row)
    summed = jnp.exp(batch - top)
    for row in lse:
        summed = summed + jnp.exp(row - top)
    log_total = top + jnp.log(summed)
    total_ref[...] = log_total
    for k in range(copies_ref.shape[0]):
        copies_ref[k] = log_total
    loss_ref[...] = log_total - stat_ref[1:2, :]


def item_kernel(*refs):
    place_ref, *g_refs, lt_ref, q_ref, it_ref, ng_ref, sh_ref, item_ref, neg_ref = refs
    rows = q_ref.shape[0]
    here = place_ref[2]
    near = g_refs[0].shape[0]
    peers = sum(ref.shape[0] for ref in g_refs)
    keys = jnp.concatenate([it_ref[...], ng_ref[...]], axis=0)
    shift = to_column(sh_ref[...])
    acc = jnp.zeros(keys.shape, F32)
    low = lax.rem(here, near)
    blocks = [(ref, k) for ref in g_refs for k in range(ref.shape[0])]
    for at in range(0, peers, 2):
        base = lax.rem(here - low - (at // near) * near + peers, peers)
        pair = blocks[at : at + 2]
        queries = jnp.concatenate([ref[k, 0:rows, :] for ref, k in pair], axis=0)
        log_total = jnp.concatenate(
            [lt_ref[pl.ds(base + (low ^ ((at + n) % near)), 1), :] for n in range(2)], axis=1
        )
        w = jnp.exp(dot_rows(keys, queries) + shift - log_total).astype(BF16)
        acc = acc + dot_plain(w, queries)
    item_ref[...] = acc[0:rows, :] - q_ref[...].astype(F32)
    neg_ref[...] = acc[rows:, :]


def query_kernel(parts_ref, lt_ref, batch_ref, stat_ref, it_ref, out_ref):
    log_total = lt_ref[...]
    rows = log_total.shape[1]
    out = batch_ref[...] * to_column(jnp.exp(stat_ref[0:1, :] - log_total))
    for k in range(parts_ref.shape[0]):
        share = to_column(jnp.exp(joined(parts_ref[k, rows : rows + 16, 0:rows]) - log_total))
        out = out + parts_ref[k, 0:rows, :].astype(F32) * share
    out_ref[...] = out - it_ref[...].astype(F32)


def local(
    query_vectors,
    item_vectors,
    negative_vectors,
    item_ids,
    negative_ids,
    negative_counts,
    memory,
    owners,
    memory_slots,
):
    rows, width = query_vectors.shape
    negatives = negative_vectors.shape[0]
    keys = rows + negatives
    mem = memory[0]
    group = lax.axis_size("dp")
    shards = lax.axis_size("zh")
    depth = shards * lax.axis_size("zl")
    cycle = depth * lax.axis_size("yh")
    column = ("yh", "zh", "zl")

    def beside(block, over, by):
        route = [
            (y * depth + z, ((y + over) % 2) * depth + (z ^ by))
            for y in range(cycle // depth)
            for z in range(depth)
        ]
        return lax.ppermute(block, column, route)

    place = jnp.stack([lax.axis_index("yh"), lax.axis_index("zl"), lax.axis_index("dp")])
    capacity = max(2, 2 * rows // cycle)
    held = mem.shape[0]
    span = shards * capacity * 3 // 2
    block, copies, shift, z_sent, y_sent, own_items = call(
        lambda *refs: prepare_kernel(capacity, group, *refs),
        (
            place,
            query_vectors,
            item_vectors,
            negative_vectors,
            item_ids[None, :],
            negative_ids[None, :],
            negative_counts[None, :],
            owners.reshape(1, rows),
            memory_slots[None, :],
            mem,
        ),
        (
            jax.ShapeDtypeStruct((rows + keys + 16, width), BF16),
            jax.ShapeDtypeStruct((shards, rows, width), BF16),
            jax.ShapeDtypeStruct((1, keys), F32),
            jax.ShapeDtypeStruct((held + 2 * span, width), BF16),
            jax.ShapeDtypeStruct((held + span, width), BF16),
            jax.ShapeDtypeStruct((span, width), BF16),
        ),
        "prepare",
    )
    near = 4
    near_blocks = [block] + [
        lax.ppermute(block, "dp", [(i, i ^ k) for i in range(group)]) for k in range(1, near)
    ]
    pair_blocks = jnp.stack(near_blocks)
    z_rows = beside(z_sent, 0, 1)
    y_rows = beside(y_sent, 1, 0)
    copies, z_rows, pair_blocks = lax.optimization_barrier((copies, z_rows, pair_blocks))
    zy_rows = beside(z_rows[: held + span], 1, 0)
    memory_blocks = [own_items, mem, z_rows, y_rows, zy_rows]
    arrived = lax.all_to_all(copies, "zh", 0, 0, tiled=True)

    def along(blocks, by):
        return lax.ppermute(blocks, "dp", [(i, (i + near * by) % group) for i in range(group)])

    before, after = along(pair_blocks, 1), along(pair_blocks, -1)
    arrived, before, after, memory_blocks = lax.optimization_barrier(
        (arrived, before, after, memory_blocks)
    )

    (parts,) = call(
        lambda *refs: memory_kernel(512, *refs),
        (arrived, *memory_blocks),
        (jax.ShapeDtypeStruct((shards, rows + 6 * capacity, width), BF16),),
        "memory",
    )
    parts, before, after = lax.optimization_barrier((parts, before, after))
    parts_back = lax.all_to_all(parts, "zh", 0, 0, tiled=True)

    group_blocks = [
        pair_blocks,
        before,
        along(before[: near // 2], 1),
        along(after[near // 2 :], -1),
        after,
    ]
    batch_part, batch_stat = call(
        batch_kernel,
        (*group_blocks, query_vectors, item_vectors, shift),
        (
            jax.ShapeDtypeStruct((rows, width), F32),
            jax.ShapeDtypeStruct((2, rows), F32),
        ),
        "batch",
        [pltpu.VMEM((group, rows, keys), F32)],
    )
    parts_back, batch_part, batch_stat = lax.optimization_barrier(
        (parts_back, batch_part, batch_stat)
    )
    log_total, total_copies, loss = call(
        total_kernel,
        (parts_back, batch_stat),
        (
            jax.ShapeDtypeStruct((1, rows), F32),
            jax.ShapeDtypeStruct((group, 1, rows), F32),
            jax.ShapeDtypeStruct((1, rows), F32),
        ),
        "total",
    )
    group_totals = lax.all_to_all(total_copies, "dp", 0, 0, tiled=True).reshape(group, rows)
    (query_grad,) = call(
        query_kernel,
        (parts_back, log_total, batch_part, batch_stat, item_vectors),
        (jax.ShapeDtypeStruct((rows, width), F32),),
        "queries",
    )
    (updated,) = call(
        lambda *refs: update_kernel(rows, capacity, *refs),
        (place, parts_back, mem),
        (jax.ShapeDtypeStruct(mem.shape, BF16),),
        "update",
    )
    group_totals, query_grad, updated = lax.optimization_barrier(
        (group_totals, query_grad, updated)
    )
    item_grad, negative_grad = call(
        item_kernel,
        (
            place,
            *group_blocks,
            group_totals,
            query_vectors,
            item_vectors,
            negative_vectors,
            shift,
        ),
        (
            jax.ShapeDtypeStruct((rows, width), F32),
            jax.ShapeDtypeStruct((negatives, width), F32),
        ),
        "items",
    )
    return (loss[0], query_grad, item_grad, negative_grad, updated[None])


def solution(mesh):
    cycle, group = mesh.shape["mem"], mesh.shape["dp"]
    cut = Mesh(
        mesh.devices.reshape(2, cycle // 4, 2, group), ("yh", "zh", "zl", "dp")
    )
    spread = ("yh", "zh", "zl", "dp")
    column = ("yh", "zh", "zl")
    return jax.shard_map(
        local,
        mesh=cut,
        in_specs=(
            P(spread, None),
            P(spread, None),
            P(spread, None),
            P(spread),
            P(spread),
            P(spread),
            P("dp", column, None),
            P(spread, None),
            P(spread),
        ),
        out_specs=(
            P(spread),
            P(spread, None),
            P(spread, None),
            P(spread, None),
            P("dp", column, None),
        ),
        check_vma=False,
    )
```
